32 devices in a mesh: parts: 2 (over x), space: 16 (over z, y, core).
Axes of the slice: x: 2, y: 2, z: 4, core: 2. Of those that a mesh axis runs over, the one named last changes fastest.
Arguments:
- volume: bfloat16 [64, 16, 16, 128], P(('parts', 'space')), parts along dimension 0, may hold values from -6 to 6
- first_filter: bfloat16 [3, 3, 3, 128, 128], replicated, may hold values from -0.109375 to 0.109375
- second_filter: bfloat16 [3, 3, 3, 128, 128], replicated, may hold values from -0.109375 to 0.109375
- cotangent: bfloat16 [64, 16, 16, 128], P(('parts', 'space')), parts along dimension 0, may hold values from -0.06591797 to 0.06591797
Outputs:
- response: bfloat16 [64, 16, 16, 128], P(('parts', 'space')), parts along dimension 0
- first_grad: float32 [256, 3, 3, 3, 128], P(('parts', 'space')), parts along dimension 0
- second_grad: float32 [256, 3, 3, 3, 128], P(('parts', 'space')), parts along dimension 0
The draws below stay inside these ranges and needn't reach their ends.
There are 2 independent parts, one for each index of `parts`. The reference program is written for one: setup_inputs(seed, part) draws one part's arguments, and reference() takes and returns one part's arrays. A program takes and returns all parts, laid end to end along the dimension named above; an argument that names none is the same for every part. Nothing has to cross between parts.
All inputs are finite; a program needn't handle non-finite values.
Results may differ from the reference program's by a relative error of at most 0.0049.
Values may be sent and summed in bfloat16 or wider, within the bound.
No kernel may reach another device: no remote copies, remote signals or barrier semaphores. Data moves between devices by JAX's collectives and lax.ppermute only.
A program may use at most 64 MiB of HBM per device.

```python
import jax
import jax.numpy as jnp
from jax import lax

C = 128
CX = 16
CY = 16
NZ = 32


def spiked(drawn, own_key, source, target, blocks, factor):
    owner, partner = [(jnp.arange(drawn.shape[axis_at]) // (drawn.shape[axis_at] // blocks)).reshape([-1 if axis == axis_at else 1 for axis in range(drawn.ndim)]) for axis_at in (source, target)]
    chosen = jax.random.permutation(own_key, blocks)[partner]
    strong = (owner == chosen) | (owner == (partner + blocks // 2) % blocks)
    return jnp.where(strong, factor * drawn, drawn)


def block_scale(key, dims, pieces, smallest, largest):
    def one(axis_at, parts):
        heights = jax.random.uniform(jax.random.fold_in(jax.random.fold_in(key, 6), axis_at), (parts,), jnp.float32, smallest / len(pieces), largest / len(pieces))
        return jnp.repeat(jnp.exp(heights), dims[axis_at] // parts).reshape((-1,) + (1,) * (len(dims) - axis_at - 1))

    loudness = one(*pieces[0])
    for cut in pieces[1:]:
        loudness = loudness * one(*cut)
    return loudness


def bell_draw(stream_key, dims, scale, reach, pieces=(), held_as=jnp.bfloat16):
    gain = block_scale(stream_key, dims, pieces, -0.22, 0.18) if pieces else 1.0
    values = jax.random.normal(stream_key, dims, jnp.float32) * scale * gain
    return jnp.minimum(jnp.maximum(values, -reach), reach).astype(held_as)


def noise_with(own_key, dims, scale, reach, split, heavy, held_as=jnp.bfloat16):
    array = scale * jax.random.normal(own_key, dims, jnp.float32)
    if split:
        array = array * block_scale(own_key, dims, split, -0.22, 0.18)
    return jnp.clip(spiked(array, jax.random.fold_in(own_key, 3), *heavy), -reach, reach).astype(held_as)


def setup_inputs(seed: int = 0, part: int = 0) -> dict:
    splits = jax.random.split(jax.random.key(seed), 5)
    own_keys = jax.random.split(jax.random.fold_in(splits[4], part), 5)
    return {
        "volume": noise_with(own_keys[0], (NZ, CX, CY, C), 1.0, 6.0, ((0, 16),), (0, 3, 16, 2.0)),
        "first_filter": bell_draw(splits[1], (3, 3, 3, C, C), (27 * C) ** -0.5, 0.109375),
        "second_filter": bell_draw(splits[2], (3, 3, 3, C, C), (27 * C) ** -0.5, 0.109375),
        "cotangent": bell_draw(own_keys[3], (NZ, CX, CY, C), (1.0 / (NZ * CX * CY) ** 0.5), 0.06591797, ((0, 16),)),
    }


def spread(field):
    return jnp.pad(field, ((0, 0), (1, 1), (1, 1), (0, 0)))


def convolve(padded, weight):
    depth = padded.shape[0] - 2
    width = padded.shape[1] - 2
    height = padded.shape[2] - 2
    inner = padded.shape[3]
    total = jnp.zeros((depth * width * height, weight.shape[4]), jnp.float32)
    for plane in range(3):
        for column in range(3):
            slab = jnp.concatenate([padded[plane:plane + depth, column:column + width, lane:lane + height, :] for lane in range(3)], axis=-1)
            total = total + jnp.dot(slab.reshape(-1, 3 * inner), weight[plane, column].reshape(3 * inner, -1), preferred_element_type=jnp.float32)
    return total.reshape(depth, width, height, -1)


def weight_term(padded, grads, start, count):
    depth, width, height, outer = grads.shape
    chosen = lax.dynamic_slice_in_dim(padded, start, count, 3)
    flat = grads.reshape(-1, outer)
    blocks = []
    for plane in range(3):
        for column in range(3):
            slab = jnp.concatenate([chosen[plane:plane + depth, column:column + width, lane:lane + height, :] for lane in range(3)], axis=-1)
            term = lax.dot_general(slab.reshape(-1, 3 * count), flat, (((0,), (0,)), ((), ())), preferred_element_type=jnp.float32)
            blocks.append(term.reshape(3, count, outer))
    stacked = jnp.stack(blocks, 0).reshape(3, 3, 3, count, outer)
    return jnp.transpose(stacked, (3, 0, 1, 2, 4))


def flipped(weight):
    return jnp.swapaxes(jnp.flip(weight, (0, 1, 2)), 3, 4)


def reference(volume, first_filter, second_filter, cotangent):
    padded_in = spread(jnp.pad(volume, ((1, 1), (0, 0), (0, 0), (0, 0))))
    hidden = convolve(padded_in, first_filter)
    activated = jax.nn.silu(hidden).astype(jnp.bfloat16)
    padded_act = spread(jnp.pad(activated, ((1, 1), (0, 0), (0, 0), (0, 0))))
    response = convolve(padded_act, second_filter).astype(jnp.bfloat16)
    padded_cot = spread(jnp.pad(cotangent, ((1, 1), (0, 0), (0, 0), (0, 0))))
    act_grad = convolve(padded_cot, flipped(second_filter))
    sigma = jax.nn.sigmoid(hidden)
    hidden_grad = (act_grad * sigma * (1.0 + hidden * (1.0 - sigma))).astype(jnp.bfloat16)
    channels = volume.shape[3]
    second_grad = weight_term(padded_act, cotangent, 0, channels)
    first_grad = weight_term(padded_in, hidden_grad, 0, channels)
    return response, first_grad, second_grad
```

```python
import functools

import jax
import jax.numpy as jnp
from jax import lax
from jax.experimental import pallas as pl
from jax.experimental.pallas import tpu as pltpu
from jax.sharding import PartitionSpec as P

F32 = jnp.float32
BF16 = jnp.bfloat16
VMEM_BYTES = 40 * 2**20


def call(body, out_shape, scratch, flops, moved, name):
    return pl.pallas_call(
        body,
        out_shape=out_shape,
        scratch_shapes=scratch,
        name=name,
        compiler_params=pltpu.CompilerParams(vmem_limit_bytes=VMEM_BYTES),
        cost_estimate=pl.CostEstimate(flops=flops, bytes_accessed=moved, transcendentals=0),
    )


def place(index, size):
    return lax.rem(index, 2), lax.rem(index // 2, 2), index // 4


def edge_rows(wide):
    planes, rows, lanes, channels = wide.shape
    zero = jnp.zeros((planes, 1, lanes, channels), wide.dtype)
    wide[:, 0:1] = zero
    wide[:, rows - 1 : rows] = zero


def moved_lanes(plane):
    length = plane.shape[1]
    at = lax.broadcasted_iota(jnp.int32, plane.shape, 1)
    before = jnp.where(at == 0, 0.0, pltpu.roll(plane, 1, 1))
    after = jnp.where(at == length - 1, 0.0, pltpu.roll(plane, length - 1, 1))
    return before, after


def widen(wide, at, plane):
    rows, _, channels = plane.shape
    before, after = moved_lanes(plane.astype(F32))
    wide[at, 1 : rows + 1, :, 0:channels] = before.astype(BF16)
    wide[at, 1 : rows + 1, :, channels : 2 * channels] = plane.astype(BF16)
    wide[at, 1 : rows + 1, :, 2 * channels : 3 * channels] = after.astype(BF16)


def patch(wide, plane, planes, column):
    rows, lanes, channels = wide.shape[1] - 2, wide.shape[2], wide.shape[3]
    return wide[plane : plane + planes, column : column + rows].reshape(planes * rows * lanes, channels)


def convolve(wide, weight, planes):
    total = None
    for plane in range(3):
        for column in range(3):
            kernel = weight[plane, column]
            term = jnp.dot(
                patch(wide, plane, planes, column),
                kernel.reshape(-1, kernel.shape[-1]),
                preferred_element_type=F32,
            )
            total = term if total is None else total + term
    return total


def convolve_back(wide, weight, planes):
    channels = weight.shape[4]
    total = None
    for plane in range(3):
        for column in range(3):
            block = patch(wide, plane, planes, column)
            for lane in range(3):
                term = lax.dot_general(
                    block[:, lane * channels : (lane + 1) * channels],
                    weight[2 - plane, 2 - column, 2 - lane],
                    (((1,), (1,)), ((), ())),
                    preferred_element_type=F32,
                )
                total = term if total is None else total + term
    return total


def hidden_kernel(size, own, sib, cross, cot, cot_sib, cot_cross, first, second, out, vol_wide, cot_wide):
    core, _, _ = place(lax.axis_index("space"), size)
    for wide, mine, near, far in ((vol_wide, own, sib, cross), (cot_wide, cot, cot_sib, cot_cross)):
        edge_rows(wide)
        widen(wide, 1, mine[0])
        widen(wide, 2, mine[1])
        widen(wide, 3 * core, far[1 - core])
        widen(wide, 3 * (1 - core), near[core])
    hidden = convolve(vol_wide, first, 2)
    sigma = jax.nn.sigmoid(hidden)
    act_grad = convolve_back(cot_wide, second, 2)
    out[0:2] = (hidden * sigma).astype(BF16).reshape(own.shape)
    out[2:4] = (act_grad * sigma * (1.0 + hidden * (1.0 - sigma))).astype(BF16).reshape(own.shape)


def response_kernel(size, act, act_sib, own, cross, first, second, out, vol_wide, act_wide):
    index = lax.axis_index("space")
    core, _, _ = place(index, size)
    edge_rows(vol_wide)
    widen(vol_wide, core, cross[0])
    widen(vol_wide, core + 1, cross[1])
    widen(vol_wide, 2 * (1 - core), own[core])
    hidden = convolve(vol_wide, first, 1)
    inside = jnp.where((index == 0) | (index == size - 1), 0.0, 1.0)
    outer = hidden * jax.nn.sigmoid(hidden) * inside
    edge_rows(act_wide)
    widen(act_wide, 1, act[0])
    widen(act_wide, 2, act[1])
    widen(act_wide, 3 * core, outer.reshape(own.shape[1:]).astype(BF16))
    widen(act_wide, 3 * (1 - core), act_sib[core])
    out[...] = convolve(act_wide, second, 2).astype(BF16).reshape(out.shape)


def channel_choice(size, channels, index):
    core, pair, z = place(index, size)
    group = size // 4
    share = channels // size
    lane = lax.broadcasted_iota(jnp.int32, (channels, channels), 1) % (channels // 2)
    row = lax.broadcasted_iota(jnp.int32, (channels, channels), 0)
    half = channels // 4
    stays = lane // half
    block = (lane % half) // share
    where_z = jnp.bitwise_xor(block, z)
    where_pair = jnp.bitwise_xor(pair, 1 - stays)
    owner = (where_z * 2 + where_pair) * 2 + core
    return jnp.where(row == owner * share + lane % share, 1.0, 0.0).astype(BF16)


def narrow(wide, at, plane, choice):
    rows, lanes, channels = plane.shape
    kept = jnp.dot(plane.reshape(rows * lanes, channels), choice, preferred_element_type=F32)
    kept = kept.reshape(rows, lanes, channels)
    before, after = moved_lanes(kept)
    lane = lax.broadcasted_iota(jnp.int32, kept.shape, 2)
    wide[at, 1 : rows + 1, :, 0:channels] = jnp.where(lane < channels // 2, before, kept).astype(BF16)
    wide[at, 1 : rows + 1, :, channels : 2 * channels] = after.astype(BF16)


def weight_kernel(size, shifted_left, *refs):
    (own, sib, cross, cross_sib, four_own, four_sib, send, keep, wide, turned) = refs
    index = lax.axis_index("space")
    core, _, _ = place(index, size)
    channels = own.shape[-1]
    voxels = own.shape[1] * own.shape[2]
    choice = channel_choice(size, channels, index)
    edge_rows(wide)
    if shifted_left:
        for i in range(2):
            narrow(wide, 1 + i + 2 * core, own[i], choice)
            narrow(wide, 3 + i - 2 * core, sib[i], choice)
            turned[i + 2 * core] = four_own[i].reshape(voxels, channels).astype(F32).T.astype(BF16)
            turned[2 + i - 2 * core] = four_sib[i].reshape(voxels, channels).astype(F32).T.astype(BF16)
        narrow(wide, 5 * core, cross[1 - core], choice)
        narrow(wide, 5 * (1 - core), cross_sib[core], choice)
    else:
        for i in range(2):
            narrow(wide, i + 2 * core, four_own[i], choice)
            narrow(wide, 2 + i - 2 * core, four_sib[i], choice)
            turned[1 + i + 2 * core] = own[i].reshape(voxels, channels).astype(F32).T.astype(BF16)
            turned[3 + i - 2 * core] = sib[i].reshape(voxels, channels).astype(F32).T.astype(BF16)
        turned[5 * core] = cross[1 - core].reshape(voxels, channels).astype(F32).T.astype(BF16)
        turned[5 * (1 - core)] = cross_sib[core].reshape(voxels, channels).astype(F32).T.astype(BF16)
    half = channels // 4
    for column in range(3):
        blocks = [None, None, None]
        for at in range(wide.shape[0]):
            right = patch(wide, at, 1, column)
            if shifted_left:
                pairs = [(a, at - a) for a in range(3) if 0 <= at - a < 4]
            else:
                pairs = [(a, at - a + 2) for a in range(3)]
            left = jnp.concatenate([turned[p] for _, p in pairs], axis=0)
            term = jnp.dot(left, right, preferred_element_type=F32)
            for i, (a, _) in enumerate(pairs):
                piece = term[i * channels : (i + 1) * channels]
                blocks[a] = piece if blocks[a] is None else blocks[a] + piece
        for a in range(3):
            first = blocks[a][:, :channels].T
            second = blocks[a][:, channels:].T
            tap = (a * 3 + column) * 3
            for lane, rows in enumerate((first[: 2 * half], first[2 * half :], second[: 2 * half])):
                send[tap + lane] = rows[:half].astype(BF16)
                keep[tap + lane] = rows[half:]


def pair_sum_kernel(share, keep, got, own, *sends):
    total = keep[...] + got[...].astype(F32)
    taps, _, channels = total.shape
    for q in range(len(sends) + 1):
        block = total[:, q * share : (q + 1) * share].reshape(taps * share, channels)
        if q == 0:
            own[...] = block
        else:
            rows = sends[q - 1].shape[0]
            pad = jnp.zeros((rows - taps * share, channels), F32)
            sends[q - 1][...] = jnp.concatenate([block, pad], axis=0).astype(BF16)


def last_sum_kernel(*refs):
    own, gots, out = refs[0], refs[1:-1], refs[-1]
    rows = own.shape[0]
    total = own[...]
    for got in gots:
        total = total + got[...].astype(F32)[:rows]
    out[...] = total


def per_device(size, volume, first_filter, second_filter, cotangent):
    channels = volume.shape[3]
    share = channels // size
    group = size // 4
    planes, width, height, _ = volume.shape
    voxels = planes * width * height
    slab = volume.size * 2
    unit = 2 * voxels * 27 * channels * channels

    def pairs(move):
        return [(i, move(i)) for i in range(size)]

    across = [(i, i + 1) for i in range(1, size - 1, 2)]
    across = across + [(j, i) for i, j in across]
    sibling = pairs(lambda i: i ^ 1)

    def send(array, moves):
        return lax.ppermute(array, "space", moves)

    vol_cross = send(volume, across)
    vol_sib = send(volume, sibling)
    cot_cross = send(cotangent, across)
    cot_sib = send(cotangent, sibling)

    def wide(count, wide_channels):
        return pltpu.VMEM((count, width + 2, height, wide_channels), BF16)

    both = call(
        functools.partial(hidden_kernel, size),
        jax.ShapeDtypeStruct((2 * planes, width, height, channels), BF16),
        [wide(4, 3 * channels), wide(4, 3 * channels)],
        2 * unit,
        8 * slab + 4 * first_filter.size,
        "hidden",
    )(volume, vol_sib, vol_cross, cotangent, cot_sib, cot_cross, first_filter, second_filter)
    both_sib = send(both, sibling)
    vol_far = send(vol_cross, sibling)
    cot_far = send(cot_cross, sibling)

    response = call(
        functools.partial(response_kernel, size),
        jax.ShapeDtypeStruct(volume.shape, BF16),
        [wide(3, 3 * channels), wide(4, 3 * channels)],
        3 * unit // 2,
        6 * slab + 4 * first_filter.size,
        "response",
    )(both[:planes], both_sib[:planes], volume, vol_cross, first_filter, second_filter)

    def filter_grad(shifted_left, operands, name):
        return call(
            functools.partial(weight_kernel, size, shifted_left),
            (
                jax.ShapeDtypeStruct((27, channels // 4, channels), BF16),
                jax.ShapeDtypeStruct((27, channels // 4, channels), F32),
            ),
            [
                wide(6 if shifted_left else 4, 2 * channels),
                pltpu.VMEM((4 if shifted_left else 6, channels, width * height), BF16),
            ],
            unit,
            6 * slab,
            name,
        )(*operands)

    def pair_sum(keep, got, name):
        if share % 8:
            total = (keep + got.astype(F32)).reshape(27, group, share, channels)
            blocks = [total[:, q].reshape(27 * share, channels) for q in range(group)]
            return [blocks[0]] + [b.astype(BF16) for b in blocks[1:]]
        rows = 27 * share
        padded = -(-rows // 16) * 16
        return call(
            functools.partial(pair_sum_kernel, share),
            (jax.ShapeDtypeStruct((rows, channels), F32),)
            + (jax.ShapeDtypeStruct((padded, channels), BF16),) * (group - 1),
            [],
            keep.size,
            8 * keep.size,
            name,
        )(keep, got)

    def spread_out(blocks):
        return [
            send(block, pairs(lambda i: (((i // 4) ^ q) * 4) + i % 4))
            for q, block in enumerate(blocks[1:], 1)
        ]

    def last_sum(own, gots, name):
        if share % 8:
            total = own
            for got in gots:
                total = total + got.astype(F32)
        else:
            total = call(
                last_sum_kernel, jax.ShapeDtypeStruct(own.shape, F32), [], own.size, 16 * own.size, name
            )(own, *gots)
        return jnp.transpose(total.reshape(3, 3, 3, share, channels), (3, 0, 1, 2, 4))

    pair = pairs(lambda i: i ^ 2)
    act, act_sib = both[:planes], both_sib[:planes]
    grad, grad_sib = both[planes:], both_sib[planes:]
    send_2, keep_2 = filter_grad(False, (cotangent, cot_sib, cot_cross, cot_far, act, act_sib), "second_grad")
    got_2 = send(send_2, pair)
    send_1, keep_1 = filter_grad(True, (volume, vol_sib, vol_cross, vol_far, grad, grad_sib), "first_grad")
    got_1 = send(send_1, pair)
    blocks_2 = pair_sum(keep_2, got_2, "second_pair_sum")
    gots_2 = spread_out(blocks_2)
    blocks_1 = pair_sum(keep_1, got_1, "first_pair_sum")
    gots_1 = spread_out(blocks_1)
    second_grad = last_sum(blocks_2[0], gots_2, "second_last_sum")
    first_grad = last_sum(blocks_1[0], gots_1, "first_last_sum")
    return response, first_grad, second_grad


def solution(mesh):
    size = mesh.shape["space"]
    return jax.shard_map(
        functools.partial(per_device, size),
        mesh=mesh,
        in_specs=(
            P(("parts", "space"), None, None, None),
            P(),
            P(),
            P(("parts", "space"), None, None, None),
        ),
        out_specs=(
            P(("parts", "space"), None, None, None),
            P(("parts", "space"), None, None, None, None),
            P(("parts", "space"), None, None, None, None),
        ),
        check_vma=False,
    )
```

```python
import functools

import jax
import jax.numpy as jnp
from jax import lax
from jax.experimental import pallas as pl
from jax.experimental.pallas import tpu as pltpu
from jax.sharding import PartitionSpec as P

F32 = jnp.float32
BF16 = jnp.bfloat16
VMEM_BYTES = 40 * 2**20


def call(body, out_shape, scratch, flops, moved, name):
    return pl.pallas_call(
        body,
        out_shape=out_shape,
        scratch_shapes=scratch,
        name=name,
        compiler_params=pltpu.CompilerParams(vmem_limit_bytes=VMEM_BYTES),
        cost_estimate=pl.CostEstimate(flops=flops, bytes_accessed=moved, transcendentals=0),
    )


def place(index, size):
    return lax.rem(index, 2), lax.rem(index // 2, 2), index // 4


def edge_rows(wide):
    planes, rows, lanes, channels = wide.shape
    zero = jnp.zeros((planes, 1, lanes, channels), wide.dtype)
    wide[:, 0:1] = zero
    wide[:, rows - 1 : rows] = zero


def moved_lanes(plane):
    length = plane.shape[1]
    at = lax.broadcasted_iota(jnp.int32, plane.shape, 1)
    before = jnp.where(at == 0, 0.0, pltpu.roll(plane, 1, 1))
    after = jnp.where(at == length - 1, 0.0, pltpu.roll(plane, length - 1, 1))
    return before, after


def widen(wide, at, plane):
    rows, _, channels = plane.shape
    before, after = moved_lanes(plane.astype(F32))
    wide[at, 1 : rows + 1, :, 0:channels] = before.astype(BF16)
    wide[at, 1 : rows + 1, :, channels : 2 * channels] = plane.astype(BF16)
    wide[at, 1 : rows + 1, :, 2 * channels : 3 * channels] = after.astype(BF16)


def patch(wide, plane, planes, column):
    rows, lanes, channels = wide.shape[1] - 2, wide.shape[2], wide.shape[3]
    return wide[plane : plane + planes, column : column + rows].reshape(planes * rows * lanes, channels)


def convolve(wide, weight, planes):
    total = None
    for plane in range(3):
        for column in range(3):
            kernel = weight[plane, column]
            term = jnp.dot(
                patch(wide, plane, planes, column),
                kernel.reshape(-1, kernel.shape[-1]),
                preferred_element_type=F32,
            )
            total = term if total is None else total + term
    return total


def convolve_back(wide, weight, planes):
    channels = weight.shape[4]
    total = None
    for plane in range(3):
        for column in range(3):
            block = patch(wide, plane, planes, column)
            for lane in range(3):
                term = lax.dot_general(
                    block[:, lane * channels : (lane + 1) * channels],
                    weight[2 - plane, 2 - column, 2 - lane],
                    (((1,), (1,)), ((), ())),
                    preferred_element_type=F32,
                )
                total = term if total is None else total + term
    return total


def inner_kernel(size, vol, sib, cot, cot_sib, first, second, part, back, vol_wide, cot_wide):
    core, _, _ = place(lax.axis_index("space"), size)
    for wide, mine, near in ((vol_wide, vol, sib), (cot_wide, cot, cot_sib)):
        edge_rows(wide)
        widen(wide, 1, mine[0])
        widen(wide, 2, mine[1])
        widen(wide, 3 * (1 - core), near[core])
        wide[3 * core] = jnp.zeros(wide.shape[1:], BF16)
    part[...] = convolve(vol_wide, first, 2).reshape(part.shape)
    back[...] = convolve_back(cot_wide, second, 2).reshape(back.shape)


def hidden_kernel(size, part, back, cross, first, second, out, wide):
    core, _, _ = place(lax.axis_index("space"), size)
    edge_rows(wide)
    widen(wide, 0, cross[0])
    widen(wide, 1, cross[1])
    channels = cross.shape[-1]
    grown, grown_back = part[core], back[core]
    for column in range(3):
        block = patch(wide, 0, 1, column)
        kernel = first[2 * core, column]
        grown = grown + jnp.dot(block, kernel.reshape(-1, channels), preferred_element_type=F32)
        block = patch(wide, 1, 1, column)
        for lane in range(3):
            grown_back = grown_back + lax.dot_general(
                block[:, lane * channels : (lane + 1) * channels],
                second[2 - 2 * core, 2 - column, 2 - lane],
                (((1,), (1,)), ((), ())),
                preferred_element_type=F32,
            )
    for at, hidden, act_grad in ((core, grown, grown_back), (1 - core, part[1 - core], back[1 - core])):
        sigma = jax.nn.sigmoid(hidden)
        out[at] = (hidden * sigma).astype(BF16).reshape(out.shape[1:])
        out[2 + at] = (act_grad * sigma * (1.0 + hidden * (1.0 - sigma))).astype(BF16).reshape(out.shape[1:])


def response_kernel(size, both, both_sib, vol, cross, first, second, out, vol_wide, wide):
    index = lax.axis_index("space")
    core, _, _ = place(index, size)
    edge_rows(vol_wide)
    widen(vol_wide, 1, cross[0])
    widen(vol_wide, 2 * core, cross[2])
    widen(vol_wide, 2 * (1 - core), vol[core])
    hidden = convolve(vol_wide, first, 1)
    inside = jnp.where((index == 0) | (index == size - 1), 0.0, 1.0)
    outer = hidden * jax.nn.sigmoid(hidden) * inside
    edge_rows(wide)
    widen(wide, 1, both[0])
    widen(wide, 2, both[1])
    widen(wide, 3 * core, outer.reshape(out.shape[1:]).astype(BF16))
    widen(wide, 3 * (1 - core), both_sib[core])
    out[...] = convolve(wide, second, 2).astype(BF16).reshape(out.shape)


def channel_choice(size, channels, index):
    core, pair, z = place(index, size)
    group = size // 4
    share = channels // size
    lane = lax.broadcasted_iota(jnp.int32, (channels, channels), 1) % (channels // 2)
    row = lax.broadcasted_iota(jnp.int32, (channels, channels), 0)
    half = channels // 4
    stays = lane // half
    block = (lane % half) // share
    where_z = jnp.bitwise_xor(block, z)
    where_pair = jnp.bitwise_xor(pair, 1 - stays)
    owner = (where_z * 2 + where_pair) * 2 + core
    return jnp.where(row == owner * share + lane % share, 1.0, 0.0).astype(BF16)


def narrow(wide, at, plane, choice):
    rows, lanes, channels = plane.shape
    kept = jnp.dot(plane.reshape(rows * lanes, channels), choice, preferred_element_type=F32)
    kept = kept.reshape(rows, lanes, channels)
    before, after = moved_lanes(kept)
    lane = lax.broadcasted_iota(jnp.int32, kept.shape, 2)
    wide[at, 1 : rows + 1, :, 0:channels] = jnp.where(lane < channels // 2, before, kept).astype(BF16)
    wide[at, 1 : rows + 1, :, channels : 2 * channels] = after.astype(BF16)


def weight_kernel(size, shifted_left, *refs):
    (own, sib, cross, cross_sib, both, both_sib, send, keep, wide, turned) = refs
    index = lax.axis_index("space")
    core, _, _ = place(index, size)
    channels = own.shape[-1]
    voxels = own.shape[1] * own.shape[2]
    choice = channel_choice(size, channels, index)
    edge_rows(wide)
    outer = 0 if shifted_left else 1
    half_at = 2 if shifted_left else 0
    four_own = [both[half_at + i] for i in range(2)]
    four_sib = [both_sib[half_at + i] for i in range(2)]
    if shifted_left:
        for i in range(2):
            narrow(wide, 1 + i + 2 * core, own[i], choice)
            narrow(wide, 3 + i - 2 * core, sib[i], choice)
            turned[i + 2 * core] = four_own[i].reshape(voxels, channels).astype(F32).T.astype(BF16)
            turned[2 + i - 2 * core] = four_sib[i].reshape(voxels, channels).astype(F32).T.astype(BF16)
        narrow(wide, 5 * core, cross[outer], choice)
        narrow(wide, 5 * (1 - core), cross_sib[outer], choice)
    else:
        for i in range(2):
            narrow(wide, i + 2 * core, four_own[i], choice)
            narrow(wide, 2 + i - 2 * core, four_sib[i], choice)
            turned[1 + i + 2 * core] = own[i].reshape(voxels, channels).astype(F32).T.astype(BF16)
            turned[3 + i - 2 * core] = sib[i].reshape(voxels, channels).astype(F32).T.astype(BF16)
        turned[5 * core] = cross[outer].reshape(voxels, channels).astype(F32).T.astype(BF16)
        turned[5 * (1 - core)] = cross_sib[outer].reshape(voxels, channels).astype(F32).T.astype(BF16)
    half = channels // 4
    for column in range(3):
        blocks = [None, None, None]
        for at in range(wide.shape[0]):
            right = patch(wide, at, 1, column)
            if shifted_left:
                pairs = [(a, at - a) for a in range(3) if 0 <= at - a < 4]
            else:
                pairs = [(a, at - a + 2) for a in range(3)]
            left = jnp.concatenate([turned[p] for _, p in pairs], axis=0)
            term = jnp.dot(left, right, preferred_element_type=F32)
            for i, (a, _) in enumerate(pairs):
                piece = term[i * channels : (i + 1) * channels]
                blocks[a] = piece if blocks[a] is None else blocks[a] + piece
        for a in range(3):
            first = blocks[a][:, :channels].T
            second = blocks[a][:, channels:].T
            tap = (a * 3 + column) * 3
            for lane, rows in enumerate((first[: 2 * half], first[2 * half :], second[: 2 * half])):
                send[tap + lane] = rows[:half].astype(BF16)
                keep[tap + lane] = rows[half:]


def pair_sum_kernel(share, keep, got, own, *sends):
    total = keep[...] + got[...].astype(F32)
    taps, _, channels = total.shape
    for q in range(len(sends) + 1):
        block = total[:, q * share : (q + 1) * share].reshape(taps * share, channels)
        if q == 0:
            own[...] = block
        else:
            rows = sends[q - 1].shape[0]
            pad = jnp.zeros((rows - taps * share, channels), F32)
            sends[q - 1][...] = jnp.concatenate([block, pad], axis=0).astype(BF16)


def last_sum_kernel(*refs):
    own, gots, out = refs[0], refs[1:-1], refs[-1]
    rows = own.shape[0]
    total = own[...]
    for got in gots:
        total = total + got[...].astype(F32)[:rows]
    out[...] = total


def per_device(size, volume, first_filter, second_filter, cotangent):
    channels = volume.shape[3]
    share = channels // size
    group = size // 4
    planes, width, height, _ = volume.shape
    voxels = planes * width * height
    slab = volume.size * 2
    unit = 2 * voxels * 27 * channels * channels

    def pairs(move):
        return [(i, move(i)) for i in range(size)]

    across = [(i, i + 1) for i in range(1, size - 1, 2)]
    across = across + [(j, i) for i, j in across]
    sibling = pairs(lambda i: i ^ 1)

    def send(array, moves):
        return lax.ppermute(array, "space", moves)

    def wide(count, wide_channels):
        return pltpu.VMEM((count, width + 2, height, wide_channels), BF16)

    slab_type = jax.ShapeDtypeStruct(volume.shape, BF16)
    sums_type = jax.ShapeDtypeStruct((planes, width * height, channels), F32)
    filter_type = jax.ShapeDtypeStruct(first_filter.shape, BF16)
    weights = 2 * first_filter.size

    core = lax.rem(lax.axis_index("space"), 2)
    edge = jnp.stack(
        [
            lax.dynamic_index_in_dim(array, at, 0, False)
            for array, at in ((volume, core), (cotangent, core), (volume, 1 - core))
        ]
    )
    cross = send(edge, across)
    vol_sib = send(volume, sibling)
    cot_sib = send(cotangent, sibling)
    part, back = call(
        functools.partial(inner_kernel, size),
        (sums_type, sums_type),
        [wide(4, 3 * channels), wide(4, 3 * channels)],
        2 * unit,
        8 * slab + 2 * weights,
        "inner",
    )(volume, vol_sib, cotangent, cot_sib, first_filter, second_filter)
    both = call(
        functools.partial(hidden_kernel, size),
        jax.ShapeDtypeStruct((2 * planes, width, height, channels), BF16),
        [wide(2, 3 * channels)],
        unit // 3,
        8 * slab + 2 * weights,
        "hidden",
    )(part, back, cross, first_filter, second_filter)
    both_sib = send(both, sibling)
    cross_far = send(cross, sibling)
    response = call(
        functools.partial(response_kernel, size),
        slab_type,
        [wide(3, 3 * channels), wide(4, 3 * channels)],
        3 * unit // 2,
        6 * slab + 2 * weights,
        "response",
    )(both, both_sib, volume, cross, first_filter, second_filter)

    def filter_grad(shifted_left, operands, name):
        return call(
            functools.partial(weight_kernel, size, shifted_left),
            (
                jax.ShapeDtypeStruct((27, channels // 4, channels), BF16),
                jax.ShapeDtypeStruct((27, channels // 4, channels), F32),
            ),
            [
                wide(6 if shifted_left else 4, 2 * channels),
                pltpu.VMEM((4 if shifted_left else 6, channels, width * height), BF16),
            ],
            unit,
            6 * slab,
            name,
        )(*operands)

    def pair_sum(keep, got, name):
        if share % 8:
            total = (keep + got.astype(F32)).reshape(27, group, share, channels)
            blocks = [total[:, q].reshape(27 * share, channels) for q in range(group)]
            return [blocks[0]] + [b.astype(BF16) for b in blocks[1:]]
        rows = 27 * share
        padded = -(-rows // 16) * 16
        return call(
            functools.partial(pair_sum_kernel, share),
            (jax.ShapeDtypeStruct((rows, channels), F32),)
            + (jax.ShapeDtypeStruct((padded, channels), BF16),) * (group - 1),
            [],
            keep.size,
            8 * keep.size,
            name,
        )(keep, got)

    def spread_out(blocks):
        return [
            send(block, pairs(lambda i: (((i // 4) ^ q) * 4) + i % 4))
            for q, block in enumerate(blocks[1:], 1)
        ]

    def last_sum(own, gots, name):
        if share % 8:
            total = own
            for got in gots:
                total = total + got.astype(F32)
        else:
            total = call(
                last_sum_kernel, jax.ShapeDtypeStruct(own.shape, F32), [], own.size, 16 * own.size, name
            )(own, *gots)
        return jnp.transpose(total.reshape(3, 3, 3, share, channels), (3, 0, 1, 2, 4))

    pair = pairs(lambda i: i ^ 2)
    send_2, keep_2 = filter_grad(False, (cotangent, cot_sib, cross, cross_far, both, both_sib), "second_grad")
    got_2 = send(send_2, pair)
    send_1, keep_1 = filter_grad(True, (volume, vol_sib, cross, cross_far, both, both_sib), "first_grad")
    got_1 = send(send_1, pair)
    got_2, response = lax.optimization_barrier((got_2, response))
    blocks_2 = pair_sum(keep_2, got_2, "second_pair_sum")
    gots_2 = spread_out(blocks_2)
    blocks_1 = pair_sum(keep_1, got_1, "first_pair_sum")
    gots_1 = spread_out(blocks_1)
    second_grad = last_sum(blocks_2[0], gots_2, "second_last_sum")
    first_grad = last_sum(blocks_1[0], gots_1, "first_last_sum")
    return response, first_grad, second_grad


def solution(mesh):
    size = mesh.shape["space"]
    return jax.shard_map(
        functools.partial(per_device, size),
        mesh=mesh,
        in_specs=(
            P(("parts", "space"), None, None, None),
            P(),
            P(),
            P(("parts", "space"), None, None, None),
        ),
        out_specs=(
            P(("parts", "space"), None, None, None),
            P(("parts", "space"), None, None, None, None),
            P(("parts", "space"), None, None, None, None),
        ),
        check_vma=False,
    )
```

```python
import functools

import jax
import jax.numpy as jnp
from jax import lax
from jax.experimental import pallas as pl
from jax.experimental.pallas import tpu as pltpu
from jax.sharding import PartitionSpec as P

F32 = jnp.float32
BF16 = jnp.bfloat16
VMEM_BYTES = 40 * 2**20


def call(body, out_shape, scratch, name):
    return pl.pallas_call(
        body,
        out_shape=out_shape,
        scratch_shapes=scratch,
        name=name,
        compiler_params=pltpu.CompilerParams(vmem_limit_bytes=VMEM_BYTES),
        cost_estimate=pl.CostEstimate(flops=0, bytes_accessed=0, transcendentals=0),
    )


def core_of(size):
    index = lax.axis_index("space")
    return index, lax.rem(index, 2)


def within(index, size):
    return jnp.where((index == 0) | (index == size - 1), 0.0, 1.0)


def edge_rows(wide):
    planes, rows, lanes, channels = wide.shape
    zero = jnp.zeros((planes, 1, lanes, channels), wide.dtype)
    wide[:, 0:1] = zero
    wide[:, rows - 1 : rows] = zero


def moved_lanes(plane):
    length = plane.shape[1]
    at = lax.broadcasted_iota(jnp.int32, plane.shape, 1)
    before = jnp.where(at == 0, 0.0, pltpu.roll(plane, 1, 1))
    after = jnp.where(at == length - 1, 0.0, pltpu.roll(plane, length - 1, 1))
    return before, after


def widen(wide, at, plane):
    rows, _, channels = plane.shape
    before, after = moved_lanes(plane.astype(F32))
    wide[at, 1 : rows + 1, :, 0:channels] = before.astype(BF16)
    wide[at, 1 : rows + 1, :, channels : 2 * channels] = plane.astype(BF16)
    wide[at, 1 : rows + 1, :, 2 * channels : 3 * channels] = after.astype(BF16)


def patch(wide, plane, planes, column):
    rows, lanes, channels = wide.shape[1] - 2, wide.shape[2], wide.shape[3]
    return wide[plane : plane + planes, column : column + rows].reshape(planes * rows * lanes, channels)


def convolve(wide, weight, planes):
    total = None
    for plane in range(3):
        for column in range(3):
            kernel = weight[plane, column]
            term = jnp.dot(
                patch(wide, plane, planes, column),
                kernel.reshape(-1, kernel.shape[-1]),
                preferred_element_type=F32,
            )
            total = term if total is None else total + term
    return total


def convolve_back(wide, weight, planes):
    channels = weight.shape[4]
    total = None
    for plane in range(3):
        for column in range(3):
            block = patch(wide, plane, planes, column)
            for lane in range(3):
                term = lax.dot_general(
                    block[:, lane * channels : (lane + 1) * channels],
                    weight[2 - plane, 2 - column, 2 - lane],
                    (((1,), (1,)), ((), ())),
                    preferred_element_type=F32,
                )
                total = term if total is None else total + term
    return total


def inner_kernel(size, vol, sib, first, part, wide):
    _, core = core_of(size)
    edge_rows(wide)
    widen(wide, 1, vol[0])
    widen(wide, 2, vol[1])
    widen(wide, 3 * (1 - core), sib[core])
    wide[3 * core] = jnp.zeros(wide.shape[1:], BF16)
    part[...] = convolve(wide, first, 2).reshape(part.shape)


def hidden_kernel(size, part, cross, first, hidden, act, wide):
    index, core = core_of(size)
    edge_rows(wide)
    widen(wide, 0, cross[0].astype(F32) * within(index, size))
    grown = part[core]
    for column in range(3):
        kernel = first[2 * core, column]
        grown = grown + jnp.dot(
            patch(wide, 0, 1, column), kernel.reshape(-1, kernel.shape[-1]), preferred_element_type=F32
        )
    for at, held in ((core, grown), (1 - core, part[1 - core])):
        hidden[at] = held
        act[at] = (held * jax.nn.sigmoid(held)).astype(BF16).reshape(act.shape[1:])


def hidden_grad_kernel(size, hidden, cot, sib, cross, second, out, wide):
    index, core = core_of(size)
    edge_rows(wide)
    widen(wide, 1, cot[0])
    widen(wide, 2, cot[1])
    widen(wide, 3 * (1 - core), sib[core])
    widen(wide, 3 * core, cross[1].astype(F32) * within(index, size))
    act_grad = convolve_back(wide, second, 2)
    held = hidden[...].reshape(act_grad.shape)
    sigma = jax.nn.sigmoid(held)
    out[...] = (act_grad * sigma * (1.0 + held * (1.0 - sigma))).astype(BF16).reshape(out.shape)


def response_kernel(size, act, sib, vol, cross, first, second, out, vol_wide, wide):
    index, core = core_of(size)
    edge_rows(vol_wide)
    widen(vol_wide, 1, cross[0])
    widen(vol_wide, 2 * core, cross[2])
    widen(vol_wide, 2 * (1 - core), vol[core])
    hidden = convolve(vol_wide, first, 1)
    outer = hidden * jax.nn.sigmoid(hidden) * within(index, size)
    edge_rows(wide)
    widen(wide, 1, act[0])
    widen(wide, 2, act[1])
    widen(wide, 3 * core, outer.reshape(out.shape[1:]).astype(BF16))
    widen(wide, 3 * (1 - core), sib[core])
    out[...] = convolve(wide, second, 2).astype(BF16).reshape(out.shape)


def channel_choice(size, channels, index):
    share = channels // size
    lane = lax.broadcasted_iota(jnp.int32, (channels, channels), 1) % (channels // 2)
    row = lax.broadcasted_iota(jnp.int32, (channels, channels), 0)
    eighth = channels // 8
    move = lane // eighth * 2 + lane % eighth // share * 8
    owner = jnp.bitwise_xor(move, index)
    return jnp.where(row == owner * share + lane % share, 1.0, 0.0).astype(BF16)


def narrow(wide, at, plane, choice):
    rows, lanes, channels = plane.shape
    kept = jnp.dot(plane.astype(BF16).reshape(rows * lanes, channels), choice, preferred_element_type=F32)
    kept = kept.reshape(rows, lanes, channels)
    before, after = moved_lanes(kept)
    lane = lax.broadcasted_iota(jnp.int32, kept.shape, 2)
    wide[at, 1 : rows + 1, :, 0:channels] = jnp.where(lane < channels // 2, before, kept).astype(BF16)
    wide[at, 1 : rows + 1, :, channels : 2 * channels] = after.astype(BF16)


def turn(plane):
    return plane.reshape(-1, plane.shape[-1]).astype(F32).T.astype(BF16)


def weight_kernel(size, which, own, sib, cross, cross_sib, four, four_sib, keep, *refs):
    sends, wide, turned = refs[:-2], refs[-2], refs[-1]
    index, core = core_of(size)
    channels = own.shape[-1]
    choice = channel_choice(size, channels, index)
    edge_rows(wide)

    def six(at, plane):
        if which:
            turned[at] = turn(plane)
        else:
            narrow(wide, at, plane, choice)

    for i in range(2):
        six(1 + i + 2 * core, own[i])
        six(3 + i - 2 * core, sib[i])
        for at, plane in ((i + 2 * core, four[i]), (2 + i - 2 * core, four_sib[i])):
            if which:
                narrow(wide, at, plane, choice)
            else:
                turned[at] = turn(plane)
    six(5 * core, cross[which].astype(F32) * within(index, size))
    six(5 * (1 - core), cross_sib[which].astype(F32) * within(jnp.bitwise_xor(index, 1), size))
    half = channels // 2
    block = half // 4
    for column in range(3):
        sums = [None, None, None]
        for at in range(wide.shape[0]):
            pairs = [(a, at - a + 2 * which) for a in range(3)]
            pairs = [(a, p) for a, p in pairs if 0 <= p < turned.shape[0]]
            left = jnp.concatenate([turned[p] for _, p in pairs], axis=0)
            term = jnp.dot(left, patch(wide, at, 1, column), preferred_element_type=F32)
            for i, (a, _) in enumerate(pairs):
                piece = term[i * channels : (i + 1) * channels]
                sums[a] = piece if sums[a] is None else sums[a] + piece
        for a in range(3):
            first = sums[a][:, :channels].T
            second = sums[a][:, channels:].T
            tap = (a * 3 + column) * 3
            for lane, rows in enumerate((first[:half], first[half:], second[:half])):
                keep[tap + lane] = rows[:block]
                for d, target in enumerate(sends, 1):
                    target[tap + lane] = rows[d * block : (d + 1) * block].astype(BF16)


def near_sum_kernel(share, keep, got_a, got_b, got_c, own, *sends):
    total = keep[...]
    for got in (got_a, got_b, got_c):
        total = total + got[...].astype(F32)
    taps, _, channels = total.shape
    for q in range(len(sends) + 1):
        block = total[:, q * share : (q + 1) * share].reshape(taps * share, channels)
        if q == 0:
            own[...] = block
        else:
            rows = sends[q - 1].shape[0]
            pad = jnp.zeros((rows - taps * share, channels), F32)
            sends[q - 1][...] = jnp.concatenate([block, pad], axis=0).astype(BF16)


def last_sum_kernel(*refs):
    own, gots, out = refs[0], refs[1:-1], refs[-1]
    rows = own.shape[0]
    total = own[...]
    for got in gots:
        total = total + got[...].astype(F32)[:rows]
    out[...] = total


def per_device(parts, size, volume, first_filter, second_filter, cotangent):
    channels = volume.shape[3]
    share = channels // size
    far = size // 8
    planes, width, height, _ = volume.shape

    def pairs(move):
        return [(i, move(i)) for i in range(size)]

    links = [(part * size + i, part * size + i + 1) for part in range(parts) for i in range(1, size - 1, 2)]
    links = links + [
        (part * size + i, (part + 1) * size + i) for part in range(0, parts, 2) for i in (0, size - 1)
    ]
    across = links + [(j, i) for i, j in links]
    sibling = pairs(lambda i: i ^ 1)

    def send(array, moves):
        return lax.ppermute(array, "space", moves)

    def send_across(array):
        return lax.ppermute(array, ("parts", "space"), across)

    def wide(count, wide_channels):
        return pltpu.VMEM((count, width + 2, height, wide_channels), BF16)

    slab_type = jax.ShapeDtypeStruct(volume.shape, BF16)
    sums_type = jax.ShapeDtypeStruct((planes, width * height, channels), F32)
    filter_type = jax.ShapeDtypeStruct(first_filter.shape, BF16)

    def hop(move):
        return pairs(lambda i: i ^ move)

    core = lax.rem(lax.axis_index("space"), 2)
    edge = jnp.where(
        core == 0,
        jnp.stack([volume[0], cotangent[0], volume[1]]),
        jnp.stack([volume[1], cotangent[1], volume[0]]),
    )
    edge, late_volume, late_cotangent = lax.optimization_barrier((edge, volume, cotangent))
    cross = send_across(edge)
    vol_sib = send(late_volume, sibling)
    cot_sib = send(late_cotangent, sibling)

    def wide(count, wide_channels):
        return pltpu.VMEM((count, width + 2, height, wide_channels), BF16)

    slab_type = jax.ShapeDtypeStruct(volume.shape, BF16)
    sums_type = jax.ShapeDtypeStruct((planes, width * height, channels), F32)

    vol_sib, cot_sib = lax.optimization_barrier((vol_sib, cot_sib))
    part = call(
        functools.partial(inner_kernel, size),
        sums_type,
        [wide(4, 3 * channels)],
        "inner",
    )(volume, vol_sib, first_filter)
    cross, part = lax.optimization_barrier((cross, part))
    hidden, act = call(
        functools.partial(hidden_kernel, size),
        (sums_type, slab_type),
        [wide(1, 3 * channels)],
        "hidden",
    )(part, cross, first_filter)
    act_sib = send(act, sibling)
    late_cross, hidden = lax.optimization_barrier((cross, hidden))
    cross_far = send(late_cross, sibling)
    grad = call(
        functools.partial(hidden_grad_kernel, size),
        slab_type,
        [wide(4, 3 * channels)],
        "hidden_grad",
    )(hidden, cotangent, cot_sib, cross, second_filter)
    grad_sib = send(grad, sibling)

    block_type = jax.ShapeDtypeStruct((27, channels // 8, channels), BF16)
    keep_type = jax.ShapeDtypeStruct(block_type.shape, F32)

    def filter_grad(which, operands, name):
        keep, *blocks = call(
            functools.partial(weight_kernel, size, which),
            (keep_type,) + (block_type,) * 3,
            [
                wide(4 if which else 6, 2 * channels),
                pltpu.VMEM((6 if which else 4, channels, width * height), BF16),
            ],
            name,
        )(*operands)
        return keep, [send(blocks[d - 1], hop(2 * d)) for d in (3, 1, 2)]

    def near_sum(keep, gots, name):
        if share % 8:
            total = (keep + sum(got.astype(F32) for got in gots)).reshape(27, far, share, channels)
            blocks = [total[:, q].reshape(27 * share, channels) for q in range(far)]
            return [blocks[0]] + [b.astype(BF16) for b in blocks[1:]]
        rows = 27 * share
        padded = -(-rows // 16) * 16
        return call(
            functools.partial(near_sum_kernel, share),
            (jax.ShapeDtypeStruct((rows, channels), F32),)
            + (jax.ShapeDtypeStruct((padded, channels), BF16),) * (far - 1),
            [],
            name,
        )(keep, *gots)

    def far_hop(blocks):
        return [send(block, hop(8 * q)) for q, block in enumerate(blocks[1:], 1)]

    def last_sum(own, gots, name):
        if share % 8:
            total = own
            for got in gots:
                total = total + got.astype(F32)
        else:
            total = call(
                last_sum_kernel, jax.ShapeDtypeStruct(own.shape, F32), [], name
            )(own, *gots)
        return jnp.transpose(total.reshape(3, 3, 3, share, channels), (3, 0, 1, 2, 4))

    keep_2, gots_2 = filter_grad(1, (cotangent, cot_sib, cross, cross_far, act, act_sib), "second_grad")
    grad_sib, keep_2 = lax.optimization_barrier((grad_sib, keep_2))
    keep_1, gots_1 = filter_grad(0, (volume, vol_sib, cross, cross_far, grad, grad_sib), "first_grad")
    blocks_2 = near_sum(keep_2, gots_2, "second_near_sum")
    gots_2 = far_hop(blocks_2)
    late_act, _ = lax.optimization_barrier((act, blocks_2[0]))
    response = call(
        functools.partial(response_kernel, size),
        slab_type,
        [wide(3, 3 * channels), wide(4, 3 * channels)],
        "response",
    )(late_act, act_sib, volume, cross, first_filter, second_filter)
    keep_1, response = lax.optimization_barrier((keep_1, response))
    blocks_1 = near_sum(keep_1, gots_1, "first_near_sum")
    gots_1 = far_hop(blocks_1)
    second_grad = last_sum(blocks_2[0], gots_2, "second_last_sum")
    first_grad = last_sum(blocks_1[0], gots_1, "first_last_sum")
    return response, first_grad, second_grad


def solution(mesh):
    size = mesh.shape["space"]
    return jax.shard_map(
        functools.partial(per_device, mesh.shape["parts"], size),
        mesh=mesh,
        in_specs=(
            P(("parts", "space"), None, None, None),
            P(),
            P(),
            P(("parts", "space"), None, None, None),
        ),
        out_specs=(
            P(("parts", "space"), None, None, None),
            P(("parts", "space"), None, None, None, None),
            P(("parts", "space"), None, None, None, None),
        ),
        check_vma=False,
    )
```

```python
import functools

import jax
import jax.numpy as jnp
from jax import lax
from jax.experimental import pallas as pl
from jax.experimental.pallas import tpu as pltpu
from jax.sharding import PartitionSpec as P

F32 = jnp.float32
BF16 = jnp.bfloat16
VMEM_BYTES = 40 * 2**20


def call(body, out_shape, scratch, name):
    return pl.pallas_call(
        body,
        out_shape=out_shape,
        scratch_shapes=scratch,
        name=name,
        compiler_params=pltpu.CompilerParams(vmem_limit_bytes=VMEM_BYTES),
        cost_estimate=pl.CostEstimate(flops=0, bytes_accessed=0, transcendentals=0),
    )


def core_of(size):
    index = lax.axis_index("space")
    return index, lax.rem(index, 2)


def within(index, size):
    return jnp.where((index == 0) | (index == size - 1), 0.0, 1.0)


def edge_rows(wide):
    planes, rows, lanes, channels = wide.shape
    zero = jnp.zeros((planes, 1, lanes, channels), wide.dtype)
    wide[:, 0:1] = zero
    wide[:, rows - 1 : rows] = zero


def moved_lanes(plane):
    length = plane.shape[1]
    at = lax.broadcasted_iota(jnp.int32, plane.shape, 1)
    before = jnp.where(at == 0, 0.0, pltpu.roll(plane, 1, 1))
    after = jnp.where(at == length - 1, 0.0, pltpu.roll(plane, length - 1, 1))
    return before, after


def widen(wide, at, plane):
    rows, _, channels = plane.shape
    before, after = moved_lanes(plane.astype(F32))
    wide[at, 1 : rows + 1, :, 0:channels] = before.astype(BF16)
    wide[at, 1 : rows + 1, :, channels : 2 * channels] = plane.astype(BF16)
    wide[at, 1 : rows + 1, :, 2 * channels : 3 * channels] = after.astype(BF16)


def patch(wide, plane, planes, column):
    rows, lanes, channels = wide.shape[1] - 2, wide.shape[2], wide.shape[3]
    return wide[plane : plane + planes, column : column + rows].reshape(planes * rows * lanes, channels)


def forward(block, kernel):
    total = None
    for column in range(3):
        taps = kernel(column)
        term = jnp.dot(block(column), taps.reshape(-1, taps.shape[-1]), preferred_element_type=F32)
        total = term if total is None else total + term
    return total


def backward(block, kernel):
    total = None
    for column in range(3):
        voxels, taps = block(column), kernel(2 - column)
        channels = taps.shape[-1]
        for lane in range(3):
            term = lax.dot_general(
                voxels[:, lane * channels : (lane + 1) * channels],
                taps[2 - lane],
                (((1,), (1,)), ((), ())),
                preferred_element_type=F32,
            )
            total = term if total is None else total + term
    return total


def convolve(wide, weight, planes):
    total = None
    for plane in range(3):
        term = forward(
            lambda column: patch(wide, plane, planes, column), lambda column: weight[plane, column]
        )
        total = term if total is None else total + term
    return total


def inner_kernel(back, own, weight, part, wide):
    run = backward if back else forward
    edge_rows(wide)
    widen(wide, 0, own[0])
    widen(wide, 1, own[1])
    middle = run(lambda column: patch(wide, 0, 2, column), lambda column: weight[1, column])
    voxels = middle.shape[0] // 2
    for plane in range(2):
        tap = 2 * plane if back else 2 - 2 * plane
        side = run(lambda column: patch(wide, 1 - plane, 1, column), lambda column: weight[tap, column])
        part[plane] = middle[plane * voxels : (plane + 1) * voxels] + side


def neighbours(size, back, part, sib, cross, weight, wide):
    index, core = core_of(size)
    run = backward if back else forward
    edge_rows(wide)
    widen(wide, 0, cross.astype(F32) * within(index, size))
    widen(wide, 1, sib[core])
    for at, plane in ((core, 0), (1 - core, 1)):
        tap = 2 - 2 * at if back else 2 * at
        side = run(lambda column: patch(wide, plane, 1, column), lambda column: weight[tap, column])
        yield at, part[at] + side


def hidden_kernel(size, part, sib, cross, cot_cross, first, hidden, near, wide):
    index, core = core_of(size)
    for at, held in neighbours(size, False, part, sib, cross[1 - core], first, wide):
        hidden[at] = held
        near[at] = (held * jax.nn.sigmoid(held)).astype(BF16).reshape(near.shape[1:])
    for i, plane in enumerate((cross[1 - core], cot_cross[...])):
        near[2 + i] = (plane.astype(F32) * within(index, size)).astype(BF16)


def hidden_grad_kernel(size, hidden, part, sib, cross, second, out, wide):
    for at, act_grad in neighbours(size, True, part, sib, cross[...], second, wide):
        held = hidden[at]
        sigma = jax.nn.sigmoid(held)
        grad = act_grad * sigma * (1.0 + held * (1.0 - sigma))
        out[at] = grad.astype(BF16).reshape(out.shape[1:])


def response_kernel(size, act, sib, vol, cross, first, second, out, vol_wide, wide):
    index, core = core_of(size)
    edge_rows(vol_wide)
    widen(vol_wide, 1, act[2])
    widen(vol_wide, 2 * core, cross[core])
    widen(vol_wide, 2 * (1 - core), vol[core])
    hidden = convolve(vol_wide, first, 1)
    outer = hidden * jax.nn.sigmoid(hidden) * within(index, size)
    edge_rows(wide)
    widen(wide, 1, act[0])
    widen(wide, 2, act[1])
    widen(wide, 3 * core, outer.reshape(out.shape[1:]).astype(BF16))
    widen(wide, 3 * (1 - core), sib[core])
    out[...] = convolve(wide, second, 2).astype(BF16).reshape(out.shape)


def channel_choice(size, channels, index):
    share = channels // size
    lane = lax.broadcasted_iota(jnp.int32, (channels, channels), 1) % (channels // 2)
    row = lax.broadcasted_iota(jnp.int32, (channels, channels), 0)
    eighth = channels // 8
    move = lane // eighth * 2 + lane % eighth // share * 8
    owner = jnp.bitwise_xor(move, index)
    return jnp.where(row == owner * share + lane % share, 1.0, 0.0).astype(BF16)


def narrow(wide, at, plane, choice):
    rows, lanes, channels = plane.shape
    kept = jnp.dot(plane.reshape(rows * lanes, channels), choice, preferred_element_type=F32)
    kept = kept.reshape(rows, lanes, channels)
    before, after = moved_lanes(kept)
    lane = lax.broadcasted_iota(jnp.int32, kept.shape, 2)
    wide[at, 1 : rows + 1, :, 0:channels] = jnp.where(lane < channels // 2, before, kept).astype(BF16)
    wide[at, 1 : rows + 1, :, channels : 2 * channels] = after.astype(BF16)


def turn(plane):
    return plane.reshape(-1, plane.shape[-1]).astype(F32).T.astype(BF16)


def weight_kernel(size, which, own, sib, near, near_sib, four, four_sib, keep, *refs):
    sends, wide, turned = refs[:-2], refs[-2], refs[-1]
    index, core = core_of(size)
    channels = own.shape[-1]
    choice = channel_choice(size, channels, index)
    edge_rows(wide)

    def six(at, plane):
        if which:
            turned[at] = turn(plane)
        else:
            narrow(wide, at, plane, choice)

    for i in range(2):
        six(1 + i + 2 * core, own[i])
        six(3 + i - 2 * core, sib[i])
        for at, plane in ((i + 2 * core, four[i]), (2 + i - 2 * core, four_sib[i])):
            if which:
                narrow(wide, at, plane, choice)
            else:
                turned[at] = turn(plane)
    six(5 * core, near[2 + which])
    six(5 * (1 - core), near_sib[2 + which])
    half = channels // 2
    block = half // 4
    for column in range(3):
        sums = [None, None, None]
        for at in range(wide.shape[0]):
            pairs = [(a, at - a + 2 * which) for a in range(3)]
            pairs = [(a, p) for a, p in pairs if 0 <= p < turned.shape[0]]
            left = jnp.concatenate([turned[p] for _, p in pairs], axis=0)
            term = jnp.dot(left, patch(wide, at, 1, column), preferred_element_type=F32)
            for i, (a, _) in enumerate(pairs):
                piece = term[i * channels : (i + 1) * channels]
                sums[a] = piece if sums[a] is None else sums[a] + piece
        for a in range(3):
            first = sums[a][:, :channels].T
            second = sums[a][:, channels:].T
            tap = (a * 3 + column) * 3
            for lane, rows in enumerate((first[:half], first[half:], second[:half])):
                keep[tap + lane] = rows[:block]
                for d, target in enumerate(sends, 1):
                    target[tap + lane] = rows[d * block : (d + 1) * block].astype(BF16)


def near_sum_kernel(share, keep, got_a, got_b, got_c, own, *sends):
    total = keep[...]
    for got in (got_a, got_b, got_c):
        total = total + got[...].astype(F32)
    taps, _, channels = total.shape
    for q in range(len(sends) + 1):
        block = total[:, q * share : (q + 1) * share].reshape(taps * share, channels)
        if q == 0:
            own[...] = block
        else:
            rows = sends[q - 1].shape[0]
            pad = jnp.zeros((rows - taps * share, channels), F32)
            sends[q - 1][...] = jnp.concatenate([block, pad], axis=0).astype(BF16)


def last_sum_kernel(*refs):
    own, gots, out = refs[0], refs[1:-1], refs[-1]
    rows = own.shape[0]
    total = own[...]
    for got in gots:
        total = total + got[...].astype(F32)[:rows]
    out[...] = total


def per_device(parts, size, volume, first_filter, second_filter, cotangent):
    channels = volume.shape[3]
    share = channels // size
    far = size // 8
    planes, width, height, _ = volume.shape

    def pairs(move):
        return [(i, move(i)) for i in range(size)]

    links = [(part * size + i, part * size + i + 1) for part in range(parts) for i in range(1, size - 1, 2)]
    links = links + [
        (part * size + i, (part + 1) * size + i) for part in range(0, parts, 2) for i in (0, size - 1)
    ]
    across = links + [(j, i) for i, j in links]
    sibling = pairs(lambda i: i ^ 1)

    def send(array, moves):
        return lax.ppermute(array, "space", moves)

    def send_across(array):
        return lax.ppermute(array, ("parts", "space"), across)

    def wide(count, wide_channels):
        return pltpu.VMEM((count, width + 2, height, wide_channels), BF16)

    def hop(move):
        return pairs(lambda i: i ^ move)

    slab_type = jax.ShapeDtypeStruct(volume.shape, BF16)
    pair_type = jax.ShapeDtypeStruct((2 * planes, width, height, channels), BF16)
    sums_type = jax.ShapeDtypeStruct((planes, width * height, channels), F32)

    core = lax.rem(lax.axis_index("space"), 2)
    vol_cross = send_across(volume)
    cot_cross = send_across(jnp.where(core == 0, cotangent[0], cotangent[1]))
    vol_sib = send(volume, sibling)
    cot_sib = send(cotangent, sibling)

    def inner(back, own, weight, name):
        return call(functools.partial(inner_kernel, back), sums_type, [wide(2, 3 * channels)], name)(own, weight)

    part = inner(False, volume, first_filter, "inner")
    part_back = inner(True, cotangent, second_filter, "inner_back")
    vol_cross, cot_cross, part, part_back, vol_sib, cot_sib = lax.optimization_barrier(
        (vol_cross, cot_cross, part, part_back, vol_sib, cot_sib)
    )
    hidden, near = call(
        functools.partial(hidden_kernel, size),
        (sums_type, pair_type),
        [wide(2, 3 * channels)],
        "hidden",
    )(part, vol_sib, vol_cross, cot_cross, first_filter)
    near_sib = send(near, sibling)
    grad = call(
        functools.partial(hidden_grad_kernel, size),
        slab_type,
        [wide(2, 3 * channels)],
        "hidden_grad",
    )(hidden, part_back, cot_sib, cot_cross, second_filter)
    grad_sib = send(grad, sibling)

    block_type = jax.ShapeDtypeStruct((27, channels // 8, channels), BF16)
    keep_type = jax.ShapeDtypeStruct(block_type.shape, F32)

    def filter_grad(which, operands, name):
        keep, *blocks = call(
            functools.partial(weight_kernel, size, which),
            (keep_type,) + (block_type,) * 3,
            [
                wide(4 if which else 6, 2 * channels),
                pltpu.VMEM((6 if which else 4, channels, width * height), BF16),
            ],
            name,
        )(*operands)
        return keep, [send(blocks[d - 1], hop(2 * d)) for d in (3, 1, 2)]

    def near_sum(keep, gots, name):
        if share % 8:
            total = (keep + sum(got.astype(F32) for got in gots)).reshape(27, far, share, channels)
            blocks = [total[:, q].reshape(27 * share, channels) for q in range(far)]
            return [blocks[0]] + [b.astype(BF16) for b in blocks[1:]]
        rows = 27 * share
        padded = -(-rows // 16) * 16
        return call(
            functools.partial(near_sum_kernel, share),
            (jax.ShapeDtypeStruct((rows, channels), F32),)
            + (jax.ShapeDtypeStruct((padded, channels), BF16),) * (far - 1),
            [],
            name,
        )(keep, *gots)

    def far_hop(blocks):
        return [send(block, hop(8 * q)) for q, block in enumerate(blocks[1:], 1)]

    def last_sum(own, gots, name):
        if share % 8:
            total = own
            for got in gots:
                total = total + got.astype(F32)
        else:
            total = call(
                last_sum_kernel, jax.ShapeDtypeStruct(own.shape, F32), [], name
            )(own, *gots)
        return jnp.transpose(total.reshape(3, 3, 3, share, channels), (3, 0, 1, 2, 4))

    keep_2, gots_2 = filter_grad(1, (cotangent, cot_sib, near, near_sib, near, near_sib), "second_grad")
    grad_sib, keep_2 = lax.optimization_barrier((grad_sib, keep_2))
    keep_1, gots_1 = filter_grad(0, (volume, vol_sib, near, near_sib, grad, grad_sib), "first_grad")
    blocks_2 = near_sum(keep_2, gots_2, "second_near_sum")
    gots_2 = far_hop(blocks_2)
    late_near, _ = lax.optimization_barrier((near, gots_1[0]))
    response = call(
        functools.partial(response_kernel, size),
        slab_type,
        [wide(3, 3 * channels), wide(4, 3 * channels)],
        "response",
    )(late_near, near_sib, volume, vol_cross, first_filter, second_filter)
    keep_1, response = lax.optimization_barrier((keep_1, response))
    blocks_1 = near_sum(keep_1, gots_1, "first_near_sum")
    gots_1 = far_hop(blocks_1)
    second_grad = last_sum(blocks_2[0], gots_2, "second_last_sum")
    first_grad = last_sum(blocks_1[0], gots_1, "first_last_sum")
    return response, first_grad, second_grad


def solution(mesh):
    size = mesh.shape["space"]
    return jax.shard_map(
        functools.partial(per_device, mesh.shape["parts"], size),
        mesh=mesh,
        in_specs=(
            P(("parts", "space"), None, None, None),
            P(),
            P(),
            P(("parts", "space"), None, None, None),
        ),
        out_specs=(
            P(("parts", "space"), None, None, None),
            P(("parts", "space"), None, None, None, None),
            P(("parts", "space"), None, None, None, None),
        ),
        check_vma=False,
    )
```

```python
import functools

import jax
import jax.numpy as jnp
from jax import lax
from jax.experimental import pallas as pl
from jax.experimental.pallas import tpu as pltpu
from jax.sharding import PartitionSpec as P

F32 = jnp.float32
BF16 = jnp.bfloat16
VMEM_BYTES = 40 * 2**20


def call(body, out_shape, scratch, name):
    return pl.pallas_call(
        body,
        out_shape=out_shape,
        scratch_shapes=scratch,
        name=name,
        compiler_params=pltpu.CompilerParams(vmem_limit_bytes=VMEM_BYTES),
        cost_estimate=pl.CostEstimate(flops=0, bytes_accessed=0, transcendentals=0),
    )


def core_of(size):
    index = lax.axis_index("space")
    return index, lax.rem(index, 2)


def within(index, size):
    return jnp.where((index == 0) | (index == size - 1), 0.0, 1.0)


def edge_rows(wide):
    planes, rows, lanes, channels = wide.shape
    zero = jnp.zeros((planes, 1, lanes, channels), wide.dtype)
    wide[:, 0:1] = zero
    wide[:, rows - 1 : rows] = zero


def moved_lanes(plane):
    length = plane.shape[1]
    at = lax.broadcasted_iota(jnp.int32, plane.shape, 1)
    before = jnp.where(at == 0, 0.0, pltpu.roll(plane, 1, 1))
    after = jnp.where(at == length - 1, 0.0, pltpu.roll(plane, length - 1, 1))
    return before, after


def widen(wide, at, plane):
    rows, _, channels = plane.shape
    before, after = moved_lanes(plane.astype(F32))
    wide[at, 1 : rows + 1, :, 0:channels] = before.astype(BF16)
    wide[at, 1 : rows + 1, :, channels : 2 * channels] = plane.astype(BF16)
    wide[at, 1 : rows + 1, :, 2 * channels : 3 * channels] = after.astype(BF16)


def patch(wide, plane, planes, column):
    rows, lanes, channels = wide.shape[1] - 2, wide.shape[2], wide.shape[3]
    return wide[plane : plane + planes, column : column + rows].reshape(planes * rows * lanes, channels)


def forward(block, kernel):
    total = None
    for column in range(3):
        taps = kernel(column)
        term = jnp.dot(block(column), taps.reshape(-1, taps.shape[-1]), preferred_element_type=F32)
        total = term if total is None else total + term
    return total


def backward(block, kernel):
    total = None
    for column in range(3):
        voxels, taps = block(column), kernel(2 - column)
        channels = taps.shape[-1]
        for lane in range(3):
            term = lax.dot_general(
                voxels[:, lane * channels : (lane + 1) * channels],
                taps[2 - lane],
                (((1,), (1,)), ((), ())),
                preferred_element_type=F32,
            )
            total = term if total is None else total + term
    return total


def convolve(wide, weight, planes):
    total = None
    for plane in range(3):
        term = forward(
            lambda column: patch(wide, plane, planes, column), lambda column: weight[plane, column]
        )
        total = term if total is None else total + term
    return total


def inner_kernel(back, own, weight, part, wide):
    run = backward if back else forward
    edge_rows(wide)
    widen(wide, 0, own[0])
    widen(wide, 1, own[1])
    middle = run(lambda column: patch(wide, 0, 2, column), lambda column: weight[1, column])
    voxels = middle.shape[0] // 2
    for plane in range(2):
        tap = 2 * plane if back else 2 - 2 * plane
        side = run(lambda column: patch(wide, 1 - plane, 1, column), lambda column: weight[tap, column])
        part[plane] = middle[plane * voxels : (plane + 1) * voxels] + side


def neighbours(size, core, back, part, sib, cross, weight, wide):
    index, _ = core_of(size)
    run = backward if back else forward
    edge_rows(wide)
    widen(wide, 0, cross.astype(F32) * within(index, size))
    widen(wide, 1, sib[core])
    for at, plane in ((core, 0), (1 - core, 1)):
        tap = 2 - 2 * at if back else 2 * at
        side = run(lambda column: patch(wide, plane, 1, column), lambda column: weight[tap, column])
        yield at, part[at] + side


def hidden_kernel(size, part, sib, cross, first, hidden, near, border, wide):
    index, core = core_of(size)
    for at, held in neighbours(size, core, False, part, sib, cross[0], first, wide):
        hidden[at] = held
        act = (held * jax.nn.sigmoid(held)).astype(BF16).reshape(near.shape[1:])
        near[at] = act
        if at is core:
            border[...] = act
    for i in range(2):
        near[2 + i] = (cross[i].astype(F32) * within(index, size)).astype(BF16)


def hidden_grad_kernel(size, hidden, part, sib, cross, second, out, wide):
    for at, act_grad in neighbours(size, core_of(size)[1], True, part, sib, cross[1], second, wide):
        held = hidden[at]
        sigma = jax.nn.sigmoid(held)
        grad = act_grad * sigma * (1.0 + held * (1.0 - sigma))
        out[at] = grad.astype(BF16).reshape(out.shape[1:])


def response_kernel(size, near, near_sib, cross, second, out, wide):
    index, core = core_of(size)
    edge_rows(wide)
    widen(wide, 1, near[0])
    widen(wide, 2, near[1])
    widen(wide, 3 * core, cross[...].astype(F32) * within(index, size))
    widen(wide, 3 * (1 - core), near_sib[core])
    out[...] = convolve(wide, second, 2).astype(BF16).reshape(out.shape)


def channel_choice(size, channels, index):
    share = channels // size
    lane = lax.broadcasted_iota(jnp.int32, (channels, channels), 1) % (channels // 2)
    row = lax.broadcasted_iota(jnp.int32, (channels, channels), 0)
    eighth = channels // 8
    move = lane // eighth * 2 + lane % eighth // share * 8
    owner = jnp.bitwise_xor(move, index)
    return jnp.where(row == owner * share + lane % share, 1.0, 0.0).astype(BF16)


def narrow(wide, at, plane, choice):
    rows, lanes, channels = plane.shape
    kept = jnp.dot(plane.reshape(rows * lanes, channels), choice, preferred_element_type=F32)
    kept = kept.reshape(rows, lanes, channels)
    before, after = moved_lanes(kept)
    lane = lax.broadcasted_iota(jnp.int32, kept.shape, 2)
    wide[at, 1 : rows + 1, :, 0:channels] = jnp.where(lane < channels // 2, before, kept).astype(BF16)
    wide[at, 1 : rows + 1, :, channels : 2 * channels] = after.astype(BF16)


def turn(plane):
    return plane.reshape(-1, plane.shape[-1]).T


def weight_kernel(size, which, own, sib, near, near_sib, four, four_sib, keep, *refs):
    sends, wide, turned = refs[:-2], refs[-2], refs[-1]
    index, core = core_of(size)
    channels = own.shape[-1]
    choice = channel_choice(size, channels, index)
    edge_rows(wide)

    def six(at, plane):
        if which:
            turned[at] = turn(plane)
        else:
            narrow(wide, at, plane, choice)

    for i in range(2):
        six(1 + i + 2 * core, own[i])
        six(3 + i - 2 * core, sib[i])
        for at, plane in ((i + 2 * core, four[i]), (2 + i - 2 * core, four_sib[i])):
            if which:
                narrow(wide, at, plane, choice)
            else:
                turned[at] = turn(plane)
    six(5 * core, near[2 + which])
    six(5 * (1 - core), near_sib[2 + which])
    half = channels // 2
    block = half // 4
    for column in range(3):
        sums = [None, None, None]
        for at in range(wide.shape[0]):
            pairs = [(a, at - a + 2 * which) for a in range(3)]
            pairs = [(a, p) for a, p in pairs if 0 <= p < turned.shape[0]]
            left = jnp.concatenate([turned[p] for _, p in pairs], axis=0)
            term = jnp.dot(left, patch(wide, at, 1, column), preferred_element_type=F32)
            for i, (a, _) in enumerate(pairs):
                piece = term[i * channels : (i + 1) * channels]
                sums[a] = piece if sums[a] is None else sums[a] + piece
        for a in range(3):
            first = sums[a][:, :channels].T
            second = sums[a][:, channels:].T
            tap = (a * 3 + column) * 3
            for lane, rows in enumerate((first[:half], first[half:], second[:half])):
                keep[tap + lane] = rows[:block]
                for d, target in enumerate(sends, 1):
                    target[tap + lane] = rows[d * block : (d + 1) * block].astype(BF16)


def near_sum_kernel(share, keep, got_a, got_b, got_c, own, *sends):
    total = keep[...]
    for got in (got_a, got_b, got_c):
        total = total + got[...].astype(F32)
    taps, _, channels = total.shape
    for q in range(len(sends) + 1):
        block = total[:, q * share : (q + 1) * share].reshape(taps * share, channels)
        if q == 0:
            own[...] = block
        else:
            rows = sends[q - 1].shape[0]
            pad = jnp.zeros((rows - taps * share, channels), F32)
            sends[q - 1][...] = jnp.concatenate([block, pad], axis=0).astype(BF16)


def last_sum_kernel(*refs):
    own, gots, out = refs[0], refs[1:-1], refs[-1]
    rows = own.shape[0]
    total = own[...]
    for got in gots:
        total = total + got[...].astype(F32)[:rows]
    out[...] = total


def per_device(parts, size, volume, first_filter, second_filter, cotangent):
    channels = volume.shape[3]
    share = channels // size
    far = size // 8
    planes, width, height, _ = volume.shape

    def pairs(move):
        return [(i, move(i)) for i in range(size)]

    links = [(part * size + i, part * size + i + 1) for part in range(parts) for i in range(1, size - 1, 2)]
    links = links + [
        (part * size + i, (part + 1) * size + i) for part in range(0, parts, 2) for i in (0, size - 1)
    ]
    across = links + [(j, i) for i, j in links]
    sibling = pairs(lambda i: i ^ 1)

    def send(array, moves):
        return lax.ppermute(array, "space", moves)

    def send_across(array):
        return lax.ppermute(array, ("parts", "space"), across)

    def wide(count, wide_channels):
        return pltpu.VMEM((count, width + 2, height, wide_channels), BF16)

    slab_type = jax.ShapeDtypeStruct(volume.shape, BF16)
    sums_type = jax.ShapeDtypeStruct((planes, width * height, channels), F32)
    pair_type = jax.ShapeDtypeStruct((2 * planes, width, height, channels), BF16)

    def hop(move):
        return pairs(lambda i: i ^ move)

    core = lax.rem(lax.axis_index("space"), 2)
    edge = jnp.where(
        core == 0,
        jnp.stack([volume[0], cotangent[0]]),
        jnp.stack([volume[1], cotangent[1]]),
    )
    edge, late_volume, late_cotangent = lax.optimization_barrier((edge, volume, cotangent))
    cross = send_across(edge)
    vol_sib = send(late_volume, sibling)
    cot_sib = send(late_cotangent, sibling)

    def inner(back, own, weight, name):
        return call(functools.partial(inner_kernel, back), sums_type, [wide(2, 3 * channels)], name)(own, weight)

    part = inner(False, volume, first_filter, "inner")
    part_back = inner(True, cotangent, second_filter, "inner_back")
    cross, part, part_back, vol_sib, cot_sib = lax.optimization_barrier(
        (cross, part, part_back, vol_sib, cot_sib)
    )
    hidden, near, border = call(
        functools.partial(hidden_kernel, size),
        (sums_type, pair_type, jax.ShapeDtypeStruct(volume.shape[1:], BF16)),
        [wide(2, 3 * channels)],
        "hidden",
    )(part, vol_sib, cross, first_filter)
    near_sib = send(near, sibling)
    grad = call(
        functools.partial(hidden_grad_kernel, size),
        slab_type,
        [wide(2, 3 * channels)],
        "hidden_grad",
    )(hidden, part_back, cot_sib, cross, second_filter)
    grad_sib = send(grad, sibling)

    block_type = jax.ShapeDtypeStruct((27, channels // 8, channels), BF16)
    keep_type = jax.ShapeDtypeStruct(block_type.shape, F32)

    def filter_grad(which, operands, name):
        keep, *blocks = call(
            functools.partial(weight_kernel, size, which),
            (keep_type,) + (block_type,) * 3,
            [
                wide(4 if which else 6, 2 * channels),
                pltpu.VMEM((6 if which else 4, channels, width * height), BF16),
            ],
            name,
        )(*operands)
        return keep, blocks

    def near_hop(blocks):
        return [send(blocks[d - 1], hop(2 * d)) for d in (3, 1, 2)]

    def near_sum(keep, gots, name):
        if share % 8:
            total = (keep + sum(got.astype(F32) for got in gots)).reshape(27, far, share, channels)
            blocks = [total[:, q].reshape(27 * share, channels) for q in range(far)]
            return [blocks[0]] + [b.astype(BF16) for b in blocks[1:]]
        rows = 27 * share
        padded = -(-rows // 16) * 16
        return call(
            functools.partial(near_sum_kernel, share),
            (jax.ShapeDtypeStruct((rows, channels), F32),)
            + (jax.ShapeDtypeStruct((padded, channels), BF16),) * (far - 1),
            [],
            name,
        )(keep, *gots)

    def far_hop(blocks):
        return [send(block, hop(8 * q)) for q, block in enumerate(blocks[1:], 1)]

    def last_sum(own, gots, name):
        if share % 8:
            total = own
            for got in gots:
                total = total + got.astype(F32)
        else:
            total = call(
                last_sum_kernel, jax.ShapeDtypeStruct(own.shape, F32), [], name
            )(own, *gots)
        return jnp.transpose(total.reshape(3, 3, 3, share, channels), (3, 0, 1, 2, 4))

    keep_2, blocks_2 = filter_grad(1, (cotangent, cot_sib, near, near_sib, near, near_sib), "second_grad")
    grad_sib, keep_2 = lax.optimization_barrier((grad_sib, keep_2))
    gots_2 = near_hop(blocks_2)
    keep_1, blocks_1 = filter_grad(0, (volume, vol_sib, near, near_sib, grad, grad_sib), "first_grad")
    gots_1 = near_hop(blocks_1)
    blocks_2 = near_sum(keep_2, gots_2, "second_near_sum")
    gots_2 = far_hop(blocks_2)
    border, _ = lax.optimization_barrier((border, blocks_2[0]))
    act_cross = send_across(border)
    keep_1, _ = lax.optimization_barrier((keep_1, blocks_2[0]))
    blocks_1 = near_sum(keep_1, gots_1, "first_near_sum")
    gots_1 = far_hop(blocks_1)
    act_cross, _ = lax.optimization_barrier((act_cross, blocks_1[0]))
    response = call(
        functools.partial(response_kernel, size),
        slab_type,
        [wide(4, 3 * channels)],
        "response",
    )(near, near_sib, act_cross, second_filter)
    first_own, response = lax.optimization_barrier((blocks_1[0], response))
    second_grad = last_sum(blocks_2[0], gots_2, "second_last_sum")
    first_grad = last_sum(first_own, gots_1, "first_last_sum")
    return response, first_grad, second_grad


def solution(mesh):
    size = mesh.shape["space"]
    return jax.shard_map(
        functools.partial(per_device, mesh.shape["parts"], size),
        mesh=mesh,
        in_specs=(
            P(("parts", "space"), None, None, None),
            P(),
            P(),
            P(("parts", "space"), None, None, None),
        ),
        out_specs=(
            P(("parts", "space"), None, None, None),
            P(("parts", "space"), None, None, None, None),
            P(("parts", "space"), None, None, None, None),
        ),
        check_vma=False,
    )
```

```python
import functools

import jax
import jax.numpy as jnp
from jax import lax
from jax.experimental import pallas as pl
from jax.experimental.pallas import tpu as pltpu
from jax.sharding import PartitionSpec as P

F32 = jnp.float32
BF16 = jnp.bfloat16
VMEM_BYTES = 40 * 2**20


def call(body, out_shape, scratch, name):
    return pl.pallas_call(
        body,
        out_shape=out_shape,
        scratch_shapes=scratch,
        name=name,
        compiler_params=pltpu.CompilerParams(vmem_limit_bytes=VMEM_BYTES),
        cost_estimate=pl.CostEstimate(flops=0, bytes_accessed=0, transcendentals=0),
    )


def core_of(size):
    index = lax.axis_index("space")
    return index, lax.rem(index, 2)


def within(index, size):
    return jnp.where((index == 0) | (index == size - 1), 0.0, 1.0)


def edge_rows(wide):
    planes, rows, lanes, channels = wide.shape
    zero = jnp.zeros((planes, 1, lanes, channels), wide.dtype)
    wide[:, 0:1] = zero
    wide[:, rows - 1 : rows] = zero


def moved_lanes(plane):
    length = plane.shape[1]
    at = lax.broadcasted_iota(jnp.int32, plane.shape, 1)
    before = jnp.where(at == 0, 0.0, pltpu.roll(plane, 1, 1))
    after = jnp.where(at == length - 1, 0.0, pltpu.roll(plane, length - 1, 1))
    return before, after


def widen(wide, at, plane):
    rows, _, channels = plane.shape
    before, after = moved_lanes(plane.astype(F32))
    wide[at, 1 : rows + 1, :, 0:channels] = before.astype(BF16)
    wide[at, 1 : rows + 1, :, channels : 2 * channels] = plane.astype(BF16)
    wide[at, 1 : rows + 1, :, 2 * channels : 3 * channels] = after.astype(BF16)


def patch(wide, plane, planes, column):
    rows, lanes, channels = wide.shape[1] - 2, wide.shape[2], wide.shape[3]
    return wide[plane : plane + planes, column : column + rows].reshape(planes * rows * lanes, channels)


def forward(block, kernel):
    total = None
    for column in range(3):
        taps = kernel(column)
        term = jnp.dot(block(column), taps.reshape(-1, taps.shape[-1]), preferred_element_type=F32)
        total = term if total is None else total + term
    return total


def backward(block, kernel):
    total = None
    for column in range(3):
        voxels, taps = block(column), kernel(2 - column)
        channels = taps.shape[-1]
        for lane in range(3):
            term = lax.dot_general(
                voxels[:, lane * channels : (lane + 1) * channels],
                taps[2 - lane],
                (((1,), (1,)), ((), ())),
                preferred_element_type=F32,
            )
            total = term if total is None else total + term
    return total


def convolve(wide, weight, planes):
    total = None
    for plane in range(3):
        term = forward(
            lambda column: patch(wide, plane, planes, column), lambda column: weight[plane, column]
        )
        total = term if total is None else total + term
    return total


def inner_kernel(back, own, weight, part, wide):
    run = backward if back else forward
    edge_rows(wide)
    widen(wide, 0, own[0])
    widen(wide, 1, own[1])
    middle = run(lambda column: patch(wide, 0, 2, column), lambda column: weight[1, column])
    voxels = middle.shape[0] // 2
    for plane in range(2):
        tap = 2 * plane if back else 2 - 2 * plane
        side = run(lambda column: patch(wide, 1 - plane, 1, column), lambda column: weight[tap, column])
        part[plane] = middle[plane * voxels : (plane + 1) * voxels] + side


def neighbours(size, core, back, part, sib, cross, weight, wide):
    index, _ = core_of(size)
    run = backward if back else forward
    edge_rows(wide)
    widen(wide, 0, cross.astype(F32) * within(index, size))
    widen(wide, 1, sib[core])
    for at, plane in ((core, 0), (1 - core, 1)):
        tap = 2 - 2 * at if back else 2 * at
        side = run(lambda column: patch(wide, plane, 1, column), lambda column: weight[tap, column])
        yield at, part[at] + side


def hidden_kernel(size, part, sib, cross, first, hidden, near, border, wide):
    index, core = core_of(size)
    for at, held in neighbours(size, core, False, part, sib, cross[0], first, wide):
        hidden[at] = held
        act = (held * jax.nn.sigmoid(held)).astype(BF16).reshape(near.shape[1:])
        near[at] = act
        if at is core:
            border[...] = act
    for i in range(2):
        near[2 + i] = (cross[i].astype(F32) * within(index, size)).astype(BF16)


def hidden_grad_kernel(size, hidden, part, sib, cross, second, out, wide):
    for at, act_grad in neighbours(size, core_of(size)[1], True, part, sib, cross[1], second, wide):
        held = hidden[at]
        sigma = jax.nn.sigmoid(held)
        grad = act_grad * sigma * (1.0 + held * (1.0 - sigma))
        out[at] = grad.astype(BF16).reshape(out.shape[1:])


def response_kernel(size, near, near_sib, cross, second, out, wide):
    index, core = core_of(size)
    edge_rows(wide)
    widen(wide, 1, near[0])
    widen(wide, 2, near[1])
    widen(wide, 3 * core, cross[...].astype(F32) * within(index, size))
    widen(wide, 3 * (1 - core), near_sib[core])
    out[...] = convolve(wide, second, 2).astype(BF16).reshape(out.shape)


def channel_choice(size, channels, index):
    share = channels // size
    lane = lax.broadcasted_iota(jnp.int32, (channels, channels), 1) % (channels // 2)
    row = lax.broadcasted_iota(jnp.int32, (channels, channels), 0)
    eighth = channels // 8
    move = lane // eighth * 2 + lane % eighth // share * 8
    owner = jnp.bitwise_xor(move, index)
    return jnp.where(row == owner * share + lane % share, 1.0, 0.0).astype(BF16)


def narrow(wide, at, plane, choice):
    rows, lanes, channels = plane.shape
    kept = jnp.dot(plane.reshape(rows * lanes, channels), choice, preferred_element_type=F32)
    kept = kept.reshape(rows, lanes, channels)
    before, after = moved_lanes(kept)
    lane = lax.broadcasted_iota(jnp.int32, kept.shape, 2)
    wide[at, 1 : rows + 1, :, 0:channels] = jnp.where(lane < channels // 2, before, kept).astype(BF16)
    wide[at, 1 : rows + 1, :, channels : 2 * channels] = after.astype(BF16)


def turn(plane):
    return plane.reshape(-1, plane.shape[-1]).T


def weight_kernel(size, which, own, sib, near, near_sib, four, four_sib, keep, *refs):
    sends, wide, turned = refs[:-2], refs[-2], refs[-1]
    index, core = core_of(size)
    channels = own.shape[-1]
    choice = channel_choice(size, channels, index)
    edge_rows(wide)

    def six(at, plane):
        if which:
            turned[at] = turn(plane)
        else:
            narrow(wide, at, plane, choice)

    for i in range(2):
        six(1 + i + 2 * core, own[i])
        six(3 + i - 2 * core, sib[i])
        for at, plane in ((i + 2 * core, four[i]), (2 + i - 2 * core, four_sib[i])):
            if which:
                narrow(wide, at, plane, choice)
            else:
                turned[at] = turn(plane)
    six(5 * core, near[2 + which])
    six(5 * (1 - core), near_sib[2 + which])
    half = channels // 2
    block = half // 4
    for column in range(3):
        sums = [None, None, None]
        for at in range(wide.shape[0]):
            pairs = [(a, at - a + 2 * which) for a in range(3)]
            pairs = [(a, p) for a, p in pairs if 0 <= p < turned.shape[0]]
            left = jnp.concatenate([turned[p] for _, p in pairs], axis=0)
            term = jnp.dot(left, patch(wide, at, 1, column), preferred_element_type=F32)
            for i, (a, _) in enumerate(pairs):
                piece = term[i * channels : (i + 1) * channels]
                sums[a] = piece if sums[a] is None else sums[a] + piece
        for a in range(3):
            first = sums[a][:, :channels].T
            second = sums[a][:, channels:].T
            tap = (a * 3 + column) * 3
            for lane, rows in enumerate((first[:half], first[half:], second[:half])):
                keep[tap + lane] = rows[:block]
                for d, target in enumerate(sends, 1):
                    target[tap + lane] = rows[d * block : (d + 1) * block].astype(BF16)


def half_products(size, index, away, slab, other, border, input_planes, wide, turned):
    channels = slab.shape[-1]
    side = jnp.bitwise_xor(lax.rem(index, 2), away)
    choice = channel_choice(size, channels, index)
    edge_rows(wide)
    for i in range(2):
        narrow(wide, i, input_planes[i], choice)
        turned[1 + i] = turn(slab[i])
    turned[3 * side] = turn(border)
    turned[3 * (1 - side)] = turn(other[side])
    left = jnp.concatenate(
        [jnp.concatenate([turned[i + 2 - a] for a in range(3)], axis=0) for i in range(2)], axis=1
    )
    return [
        jnp.dot(left, patch(wide, 0, 2, column), preferred_element_type=F32) for column in range(3)
    ]


def second_own_kernel(size, cot, cot_sib, near, out, wide, turned):
    index, _ = core_of(size)
    sums = half_products(size, index, 0, cot, cot_sib, near[3], near, wide, turned)
    for column in range(3):
        out[column] = sums[column]


def second_rest_kernel(size, cot, cot_sib, near_sib, own, keep, *refs):
    sends, wide, turned = refs[:-2], refs[-2], refs[-1]
    index, _ = core_of(size)
    channels = cot.shape[-1]
    sums = half_products(size, index, 1, cot_sib, cot, near_sib[3], near_sib, wide, turned)
    half = channels // 2
    block = half // 4
    for column in range(3):
        total = sums[column] + own[column]
        for a in range(3):
            rows_a = total[a * channels : (a + 1) * channels]
            first = rows_a[:, :channels].T
            second = rows_a[:, channels:].T
            tap = (a * 3 + column) * 3
            for lane, rows in enumerate((first[:half], first[half:], second[:half])):
                keep[tap + lane] = rows[:block]
                for d, target in enumerate(sends, 1):
                    target[tap + lane] = rows[d * block : (d + 1) * block].astype(BF16)


def near_sum_kernel(share, keep, got_a, got_b, got_c, own, *sends):
    total = keep[...]
    for got in (got_a, got_b, got_c):
        total = total + got[...].astype(F32)
    taps, _, channels = total.shape
    for q in range(len(sends) + 1):
        block = total[:, q * share : (q + 1) * share].reshape(taps * share, channels)
        if q == 0:
            own[...] = block
        else:
            rows = sends[q - 1].shape[0]
            pad = jnp.zeros((rows - taps * share, channels), F32)
            sends[q - 1][...] = jnp.concatenate([block, pad], axis=0).astype(BF16)


def last_sum_kernel(*refs):
    own, gots, out = refs[0], refs[1:-1], refs[-1]
    rows = own.shape[0]
    total = own[...]
    for got in gots:
        total = total + got[...].astype(F32)[:rows]
    out[...] = total


def per_device(parts, size, volume, first_filter, second_filter, cotangent):
    channels = volume.shape[3]
    share = channels // size
    far = size // 8
    planes, width, height, _ = volume.shape

    def pairs(move):
        return [(i, move(i)) for i in range(size)]

    links = [(part * size + i, part * size + i + 1) for part in range(parts) for i in range(1, size - 1, 2)]
    links = links + [
        (part * size + i, (part + 1) * size + i) for part in range(0, parts, 2) for i in (0, size - 1)
    ]
    across = links + [(j, i) for i, j in links]
    sibling = pairs(lambda i: i ^ 1)

    def send(array, moves):
        return lax.ppermute(array, "space", moves)

    def send_across(array):
        return lax.ppermute(array, ("parts", "space"), across)

    def wide(count, wide_channels):
        return pltpu.VMEM((count, width + 2, height, wide_channels), BF16)

    slab_type = jax.ShapeDtypeStruct(volume.shape, BF16)
    sums_type = jax.ShapeDtypeStruct((planes, width * height, channels), F32)
    pair_type = jax.ShapeDtypeStruct((2 * planes, width, height, channels), BF16)

    def hop(move):
        return pairs(lambda i: i ^ move)

    core = lax.rem(lax.axis_index("space"), 2)
    edge = jnp.where(
        core == 0,
        jnp.stack([volume[0], cotangent[0]]),
        jnp.stack([volume[1], cotangent[1]]),
    )
    edge, late_volume, late_cotangent = lax.optimization_barrier((edge, volume, cotangent))
    cross = send_across(edge)
    vol_sib = send(late_volume, sibling)
    cot_sib = send(late_cotangent, sibling)

    def inner(back, own, weight, name):
        return call(functools.partial(inner_kernel, back), sums_type, [wide(2, 3 * channels)], name)(own, weight)

    part = inner(False, volume, first_filter, "inner")
    part_back = inner(True, cotangent, second_filter, "inner_back")
    cross, part, part_back, vol_sib, cot_sib = lax.optimization_barrier(
        (cross, part, part_back, vol_sib, cot_sib)
    )
    hidden, near, border = call(
        functools.partial(hidden_kernel, size),
        (sums_type, pair_type, jax.ShapeDtypeStruct(volume.shape[1:], BF16)),
        [wide(2, 3 * channels)],
        "hidden",
    )(part, vol_sib, cross, first_filter)
    near_sib = send(near, sibling)
    grad = call(
        functools.partial(hidden_grad_kernel, size),
        slab_type,
        [wide(2, 3 * channels)],
        "hidden_grad",
    )(hidden, part_back, cot_sib, cross, second_filter)
    grad_sib = send(grad, sibling)

    block_type = jax.ShapeDtypeStruct((27, channels // 8, channels), BF16)
    keep_type = jax.ShapeDtypeStruct(block_type.shape, F32)

    def filter_grad(which, operands, name):
        keep, *blocks = call(
            functools.partial(weight_kernel, size, which),
            (keep_type,) + (block_type,) * 3,
            [
                wide(4 if which else 6, 2 * channels),
                pltpu.VMEM((6 if which else 4, channels, width * height), BF16),
            ],
            name,
        )(*operands)
        return keep, blocks

    def near_hop(blocks):
        return [send(blocks[d - 1], hop(2 * d)) for d in (3, 1, 2)]

    def near_sum(keep, gots, name):
        if share % 8:
            total = (keep + sum(got.astype(F32) for got in gots)).reshape(27, far, share, channels)
            blocks = [total[:, q].reshape(27 * share, channels) for q in range(far)]
            return [blocks[0]] + [b.astype(BF16) for b in blocks[1:]]
        rows = 27 * share
        padded = -(-rows // 16) * 16
        return call(
            functools.partial(near_sum_kernel, share),
            (jax.ShapeDtypeStruct((rows, channels), F32),)
            + (jax.ShapeDtypeStruct((padded, channels), BF16),) * (far - 1),
            [],
            name,
        )(keep, *gots)

    def far_hop(blocks):
        return [send(block, hop(8 * q)) for q, block in enumerate(blocks[1:], 1)]

    def last_sum(own, gots, name):
        if share % 8:
            total = own
            for got in gots:
                total = total + got.astype(F32)
        else:
            total = call(
                last_sum_kernel, jax.ShapeDtypeStruct(own.shape, F32), [], name
            )(own, *gots)
        return jnp.transpose(total.reshape(3, 3, 3, share, channels), (3, 0, 1, 2, 4))

    halves = [wide(2, 2 * channels), pltpu.VMEM((4, channels, width * height), BF16)]
    own_2 = call(
        functools.partial(second_own_kernel, size),
        jax.ShapeDtypeStruct((3, 3 * channels, 2 * channels), F32),
        halves,
        "second_own",
    )(cotangent, cot_sib, near)
    keep_2, *blocks_2 = call(
        functools.partial(second_rest_kernel, size),
        (keep_type,) + (block_type,) * 3,
        halves,
        "second_rest",
    )(cotangent, cot_sib, near_sib, own_2)
    grad_sib, keep_2 = lax.optimization_barrier((grad_sib, keep_2))
    gots_2 = near_hop(blocks_2)
    keep_1, blocks_1 = filter_grad(0, (volume, vol_sib, near, near_sib, grad, grad_sib), "first_grad")
    gots_1 = near_hop(blocks_1)
    blocks_2 = near_sum(keep_2, gots_2, "second_near_sum")
    gots_2 = far_hop(blocks_2)
    border, _ = lax.optimization_barrier((border, blocks_2[0]))
    act_cross = send_across(border)
    keep_1, _ = lax.optimization_barrier((keep_1, blocks_2[0]))
    blocks_1 = near_sum(keep_1, gots_1, "first_near_sum")
    gots_1 = far_hop(blocks_1)
    act_cross, _ = lax.optimization_barrier((act_cross, blocks_1[0]))
    response = call(
        functools.partial(response_kernel, size),
        slab_type,
        [wide(4, 3 * channels)],
        "response",
    )(near, near_sib, act_cross, second_filter)
    first_own, response = lax.optimization_barrier((blocks_1[0], response))
    second_grad = last_sum(blocks_2[0], gots_2, "second_last_sum")
    first_grad = last_sum(first_own, gots_1, "first_last_sum")
    return response, first_grad, second_grad


def solution(mesh):
    size = mesh.shape["space"]
    return jax.shard_map(
        functools.partial(per_device, mesh.shape["parts"], size),
        mesh=mesh,
        in_specs=(
            P(("parts", "space"), None, None, None),
            P(),
            P(),
            P(("parts", "space"), None, None, None),
        ),
        out_specs=(
            P(("parts", "space"), None, None, None),
            P(("parts", "space"), None, None, None, None),
            P(("parts", "space"), None, None, None, None),
        ),
        check_vma=False,
    )
```

```python
import functools

import jax
import jax.numpy as jnp
from jax import lax
from jax.experimental import pallas as pl
from jax.experimental.pallas import tpu as pltpu
from jax.sharding import PartitionSpec as P

F32 = jnp.float32
BF16 = jnp.bfloat16
VMEM_BYTES = 40 * 2**20


def call(body, out_shape, scratch, name):
    return pl.pallas_call(
        body,
        out_shape=out_shape,
        scratch_shapes=scratch,
        name=name,
        compiler_params=pltpu.CompilerParams(vmem_limit_bytes=VMEM_BYTES),
        cost_estimate=pl.CostEstimate(flops=0, bytes_accessed=0, transcendentals=0),
    )


def core_of(size):
    index = lax.axis_index("space")
    return index, lax.rem(index, 2)


def within(index, size):
    return jnp.where((index == 0) | (index == size - 1), 0.0, 1.0)


def edge_rows(wide):
    planes, rows, lanes, channels = wide.shape
    zero = jnp.zeros((planes, 1, lanes, channels), wide.dtype)
    wide[:, 0:1] = zero
    wide[:, rows - 1 : rows] = zero


def moved_lanes(plane):
    length = plane.shape[1]
    at = lax.broadcasted_iota(jnp.int32, plane.shape, 1)
    before = jnp.where(at == 0, 0.0, pltpu.roll(plane, 1, 1))
    after = jnp.where(at == length - 1, 0.0, pltpu.roll(plane, length - 1, 1))
    return before, after


def widen(wide, at, plane):
    rows, _, channels = plane.shape
    before, after = moved_lanes(plane.astype(F32))
    wide[at, 1 : rows + 1, :, 0:channels] = before.astype(BF16)
    wide[at, 1 : rows + 1, :, channels : 2 * channels] = plane.astype(BF16)
    wide[at, 1 : rows + 1, :, 2 * channels : 3 * channels] = after.astype(BF16)


def patch(wide, plane, planes, column):
    rows, lanes, channels = wide.shape[1] - 2, wide.shape[2], wide.shape[3]
    return wide[plane : plane + planes, column : column + rows].reshape(planes * rows * lanes, channels)


def forward(block, kernel):
    total = None
    for column in range(3):
        taps = kernel(column)
        term = jnp.dot(block(column), taps.reshape(-1, taps.shape[-1]), preferred_element_type=F32)
        total = term if total is None else total + term
    return total


def backward(block, kernel):
    total = None
    for column in range(3):
        voxels, taps = block(column), kernel(2 - column)
        channels = taps.shape[-1]
        for lane in range(3):
            term = lax.dot_general(
                voxels[:, lane * channels : (lane + 1) * channels],
                taps[2 - lane],
                (((1,), (1,)), ((), ())),
                preferred_element_type=F32,
            )
            total = term if total is None else total + term
    return total


def convolve(wide, weight, planes):
    total = None
    for plane in range(3):
        term = forward(
            lambda column: patch(wide, plane, planes, column), lambda column: weight[plane, column]
        )
        total = term if total is None else total + term
    return total


def inner_kernel(size, back, edge, rest, weight, part, wide):
    run = backward if back else forward
    edge_rows(wide)
    _, core = core_of(size)
    widen(wide, core, edge[int(back)])
    widen(wide, 1 - core, rest[int(back)])
    middle = run(lambda column: patch(wide, 0, 2, column), lambda column: weight[1, column])
    voxels = middle.shape[0] // 2
    for plane in range(2):
        tap = 2 * plane if back else 2 - 2 * plane
        side = run(lambda column: patch(wide, 1 - plane, 1, column), lambda column: weight[tap, column])
        part[plane] = middle[plane * voxels : (plane + 1) * voxels] + side


def neighbours(size, core, back, part, sib, cross, weight, wide):
    index, _ = core_of(size)
    run = backward if back else forward
    edge_rows(wide)
    widen(wide, 0, cross.astype(F32) * within(index, size))
    widen(wide, 1, sib[core])
    for at, plane in ((core, 0), (1 - core, 1)):
        tap = 2 - 2 * at if back else 2 * at
        side = run(lambda column: patch(wide, plane, 1, column), lambda column: weight[tap, column])
        yield at, part[at] + side


def hidden_kernel(size, part, sib, cross, first, hidden, near, border, wide):
    index, core = core_of(size)
    for at, held in neighbours(size, core, False, part, sib, cross[0], first, wide):
        hidden[at] = held
        act = (held * jax.nn.sigmoid(held)).astype(BF16).reshape(near.shape[1:])
        near[at] = act
        if at is core:
            border[...] = act
    for i in range(2):
        near[2 + i] = (cross[i].astype(F32) * within(index, size)).astype(BF16)


def hidden_grad_kernel(size, hidden, part, sib, cross, second, out, wide):
    for at, act_grad in neighbours(size, core_of(size)[1], True, part, sib, cross[1], second, wide):
        held = hidden[at]
        sigma = jax.nn.sigmoid(held)
        grad = act_grad * sigma * (1.0 + held * (1.0 - sigma))
        out[at] = grad.astype(BF16).reshape(out.shape[1:])


def response_kernel(size, near, near_sib, cross, second, out, wide):
    index, core = core_of(size)
    edge_rows(wide)
    widen(wide, 1, near[0])
    widen(wide, 2, near[1])
    widen(wide, 3 * core, cross[...].astype(F32) * within(index, size))
    widen(wide, 3 * (1 - core), near_sib[core])
    out[...] = convolve(wide, second, 2).astype(BF16).reshape(out.shape)


def channel_choice(size, channels, index):
    share = channels // size
    lane = lax.broadcasted_iota(jnp.int32, (channels, channels), 1) % (channels // 2)
    row = lax.broadcasted_iota(jnp.int32, (channels, channels), 0)
    eighth = channels // 8
    move = lane // eighth * 2 + lane % eighth // share * 8
    owner = jnp.bitwise_xor(move, index)
    return jnp.where(row == owner * share + lane % share, 1.0, 0.0).astype(BF16)


def narrow(wide, at, plane, choice):
    rows, lanes, channels = plane.shape
    kept = jnp.dot(plane.reshape(rows * lanes, channels), choice, preferred_element_type=F32)
    kept = kept.reshape(rows, lanes, channels)
    before, after = moved_lanes(kept)
    lane = lax.broadcasted_iota(jnp.int32, kept.shape, 2)
    wide[at, 1 : rows + 1, :, 0:channels] = jnp.where(lane < channels // 2, before, kept).astype(BF16)
    wide[at, 1 : rows + 1, :, channels : 2 * channels] = after.astype(BF16)


def turn(plane):
    return plane.reshape(-1, plane.shape[-1]).T


def weight_kernel(size, which, own, sib, near, near_sib, four, four_sib, keep, *refs):
    sends, wide, turned = refs[:-2], refs[-2], refs[-1]
    index, core = core_of(size)
    channels = own.shape[-1]
    choice = channel_choice(size, channels, index)
    edge_rows(wide)

    def six(at, plane):
        if which:
            turned[at] = turn(plane)
        else:
            narrow(wide, at, plane, choice)

    for i in range(2):
        six(1 + i + 2 * core, own[i])
        six(3 + i - 2 * core, sib[i])
        for at, plane in ((i + 2 * core, four[i]), (2 + i - 2 * core, four_sib[i])):
            if which:
                narrow(wide, at, plane, choice)
            else:
                turned[at] = turn(plane)
    six(5 * core, near[2 + which])
    six(5 * (1 - core), near_sib[2 + which])
    half = channels // 2
    block = half // 4
    for column in range(3):
        sums = [None, None, None]
        for at in range(wide.shape[0]):
            pairs = [(a, at - a + 2 * which) for a in range(3)]
            pairs = [(a, p) for a, p in pairs if 0 <= p < turned.shape[0]]
            left = jnp.concatenate([turned[p] for _, p in pairs], axis=0)
            term = jnp.dot(left, patch(wide, at, 1, column), preferred_element_type=F32)
            for i, (a, _) in enumerate(pairs):
                piece = term[i * channels : (i + 1) * channels]
                sums[a] = piece if sums[a] is None else sums[a] + piece
        for a in range(3):
            first = sums[a][:, :channels].T
            second = sums[a][:, channels:].T
            tap = (a * 3 + column) * 3
            for lane, rows in enumerate((first[:half], first[half:], second[:half])):
                keep[tap + lane] = rows[:block]
                for d, target in enumerate(sends, 1):
                    target[tap + lane] = rows[d * block : (d + 1) * block].astype(BF16)


def half_products(size, index, away, slab, other, border, input_planes, wide, turned):
    channels = slab.shape[-1]
    side = jnp.bitwise_xor(lax.rem(index, 2), away)
    choice = channel_choice(size, channels, index)
    edge_rows(wide)
    for i in range(2):
        narrow(wide, i, input_planes[i], choice)
        turned[1 + i] = turn(slab[i])
    turned[3 * side] = turn(border)
    turned[3 * (1 - side)] = turn(other[side])
    left = jnp.concatenate(
        [jnp.concatenate([turned[i + 2 - a] for a in range(3)], axis=0) for i in range(2)], axis=1
    )
    return [
        jnp.dot(left, patch(wide, 0, 2, column), preferred_element_type=F32) for column in range(3)
    ]


def second_own_kernel(size, cot, cot_sib, near, out, wide, turned):
    index, _ = core_of(size)
    sums = half_products(size, index, 0, cot, cot_sib, near[3], near, wide, turned)
    for column in range(3):
        out[column] = sums[column]


def second_rest_kernel(size, cot, cot_sib, near_sib, own, keep, *refs):
    sends, wide, turned = refs[:-2], refs[-2], refs[-1]
    index, _ = core_of(size)
    channels = cot.shape[-1]
    sums = half_products(size, index, 1, cot_sib, cot, near_sib[3], near_sib, wide, turned)
    half = channels // 2
    block = half // 4
    for column in range(3):
        total = sums[column] + own[column]
        for a in range(3):
            rows_a = total[a * channels : (a + 1) * channels]
            first = rows_a[:, :channels].T
            second = rows_a[:, channels:].T
            tap = (a * 3 + column) * 3
            for lane, rows in enumerate((first[:half], first[half:], second[:half])):
                keep[tap + lane] = rows[:block]
                for d, target in enumerate(sends, 1):
                    target[tap + lane] = rows[d * block : (d + 1) * block].astype(BF16)


def near_sum_kernel(share, keep, got_a, got_b, got_c, own, *sends):
    total = keep[...]
    for got in (got_a, got_b, got_c):
        total = total + got[...].astype(F32)
    taps, _, channels = total.shape
    for q in range(len(sends) + 1):
        block = total[:, q * share : (q + 1) * share].reshape(taps * share, channels)
        if q == 0:
            own[...] = block
        else:
            rows = sends[q - 1].shape[0]
            pad = jnp.zeros((rows - taps * share, channels), F32)
            sends[q - 1][...] = jnp.concatenate([block, pad], axis=0).astype(BF16)


def last_sum_kernel(*refs):
    own, gots, out = refs[0], refs[1:-1], refs[-1]
    rows = own.shape[0]
    total = own[...]
    for got in gots:
        total = total + got[...].astype(F32)[:rows]
    out[...] = total


def per_device(parts, size, volume, first_filter, second_filter, cotangent):
    channels = volume.shape[3]
    share = channels // size
    far = size // 8
    planes, width, height, _ = volume.shape

    def pairs(move):
        return [(i, move(i)) for i in range(size)]

    links = [(part * size + i, part * size + i + 1) for part in range(parts) for i in range(1, size - 1, 2)]
    links = links + [
        (part * size + i, (part + 1) * size + i) for part in range(0, parts, 2) for i in (0, size - 1)
    ]
    across = links + [(j, i) for i, j in links]
    sibling = pairs(lambda i: i ^ 1)

    def send(array, moves):
        return lax.ppermute(array, "space", moves)

    def send_across(array):
        return lax.ppermute(array, ("parts", "space"), across)

    def wide(count, wide_channels):
        return pltpu.VMEM((count, width + 2, height, wide_channels), BF16)

    slab_type = jax.ShapeDtypeStruct(volume.shape, BF16)
    sums_type = jax.ShapeDtypeStruct((planes, width * height, channels), F32)
    pair_type = jax.ShapeDtypeStruct((2 * planes, width, height, channels), BF16)

    def hop(move):
        return pairs(lambda i: i ^ move)

    core = lax.rem(lax.axis_index("space"), 2)
    edge = jnp.where(
        core == 0,
        jnp.stack([volume[0], cotangent[0]]),
        jnp.stack([volume[1], cotangent[1]]),
    )
    rest = jnp.where(
        core == 0,
        jnp.stack([volume[1], cotangent[1]]),
        jnp.stack([volume[0], cotangent[0]]),
    )
    cross = send_across(edge)

    def inner(back, weight, name):
        body = functools.partial(inner_kernel, size, back)
        return call(body, sums_type, [wide(2, 3 * channels)], name)(edge, rest, weight)

    part = inner(False, first_filter, "inner")
    part_back = inner(True, second_filter, "inner_back")
    late_volume, late_cotangent, part = lax.optimization_barrier((volume, cotangent, part))
    vol_sib = send(late_volume, sibling)
    cot_sib = send(late_cotangent, sibling)
    cross, part, part_back, vol_sib, cot_sib = lax.optimization_barrier(
        (cross, part, part_back, vol_sib, cot_sib)
    )
    hidden, near, border = call(
        functools.partial(hidden_kernel, size),
        (sums_type, pair_type, jax.ShapeDtypeStruct(volume.shape[1:], BF16)),
        [wide(2, 3 * channels)],
        "hidden",
    )(part, vol_sib, cross, first_filter)
    near_sib = send(near, sibling)
    grad = call(
        functools.partial(hidden_grad_kernel, size),
        slab_type,
        [wide(2, 3 * channels)],
        "hidden_grad",
    )(hidden, part_back, cot_sib, cross, second_filter)
    grad_sib = send(grad, sibling)

    block_type = jax.ShapeDtypeStruct((27, channels // 8, channels), BF16)
    keep_type = jax.ShapeDtypeStruct(block_type.shape, F32)

    def filter_grad(which, operands, name):
        keep, *blocks = call(
            functools.partial(weight_kernel, size, which),
            (keep_type,) + (block_type,) * 3,
            [
                wide(4 if which else 6, 2 * channels),
                pltpu.VMEM((6 if which else 4, channels, width * height), BF16),
            ],
            name,
        )(*operands)
        return keep, blocks

    def near_hop(blocks):
        return [send(blocks[d - 1], hop(2 * d)) for d in (3, 1, 2)]

    def near_sum(keep, gots, name):
        if share % 8:
            total = (keep + sum(got.astype(F32) for got in gots)).reshape(27, far, share, channels)
            blocks = [total[:, q].reshape(27 * share, channels) for q in range(far)]
            return [blocks[0]] + [b.astype(BF16) for b in blocks[1:]]
        rows = 27 * share
        padded = -(-rows // 16) * 16
        return call(
            functools.partial(near_sum_kernel, share),
            (jax.ShapeDtypeStruct((rows, channels), F32),)
            + (jax.ShapeDtypeStruct((padded, channels), BF16),) * (far - 1),
            [],
            name,
        )(keep, *gots)

    def far_hop(blocks):
        return [send(block, hop(8 * q)) for q, block in enumerate(blocks[1:], 1)]

    def last_sum(own, gots, name):
        if share % 8:
            total = own
            for got in gots:
                total = total + got.astype(F32)
        else:
            total = call(
                last_sum_kernel, jax.ShapeDtypeStruct(own.shape, F32), [], name
            )(own, *gots)
        return jnp.transpose(total.reshape(3, 3, 3, share, channels), (3, 0, 1, 2, 4))

    halves = [wide(2, 2 * channels), pltpu.VMEM((4, channels, width * height), BF16)]
    own_2 = call(
        functools.partial(second_own_kernel, size),
        jax.ShapeDtypeStruct((3, 3 * channels, 2 * channels), F32),
        halves,
        "second_own",
    )(cotangent, cot_sib, near)
    keep_2, *blocks_2 = call(
        functools.partial(second_rest_kernel, size),
        (keep_type,) + (block_type,) * 3,
        halves,
        "second_rest",
    )(cotangent, cot_sib, near_sib, own_2)
    grad_sib, keep_2 = lax.optimization_barrier((grad_sib, keep_2))
    gots_2 = near_hop(blocks_2)
    keep_1, blocks_1 = filter_grad(0, (volume, vol_sib, near, near_sib, grad, grad_sib), "first_grad")
    gots_1 = near_hop(blocks_1)
    blocks_2 = near_sum(keep_2, gots_2, "second_near_sum")
    gots_2 = far_hop(blocks_2)
    border, _ = lax.optimization_barrier((border, blocks_2[0]))
    act_cross = send_across(border)
    keep_1, _ = lax.optimization_barrier((keep_1, blocks_2[0]))
    blocks_1 = near_sum(keep_1, gots_1, "first_near_sum")
    gots_1 = far_hop(blocks_1)
    act_cross, _ = lax.optimization_barrier((act_cross, blocks_1[0]))
    response = call(
        functools.partial(response_kernel, size),
        slab_type,
        [wide(4, 3 * channels)],
        "response",
    )(near, near_sib, act_cross, second_filter)
    first_own, response = lax.optimization_barrier((blocks_1[0], response))
    second_grad = last_sum(blocks_2[0], gots_2, "second_last_sum")
    first_grad = last_sum(first_own, gots_1, "first_last_sum")
    return response, first_grad, second_grad


def solution(mesh):
    size = mesh.shape["space"]
    return jax.shard_map(
        functools.partial(per_device, mesh.shape["parts"], size),
        mesh=mesh,
        in_specs=(
            P(("parts", "space"), None, None, None),
            P(),
            P(),
            P(("parts", "space"), None, None, None),
        ),
        out_specs=(
            P(("parts", "space"), None, None, None),
            P(("parts", "space"), None, None, None, None),
            P(("parts", "space"), None, None, None, None),
        ),
        check_vma=False,
    )
```
